128 devices in a mesh: dp: 64 (over y, x, z_lo, core), mp: 2 (over z_hi).
Axes of the slice: x: 4, y: 4, z: 4 (z_hi: 2, z_lo: 2; z = z_hi * 2 + z_lo), core: 2. Of those that a mesh axis runs over, the one named last changes fastest.
Arguments:
- views: bfloat16 [8192, 1024], P('dp', 'mp'), may hold values from -6 to 6
- view_study: int32 [8192], P('dp'), may hold values from -1 to 1023, as said below
- pool_query: bfloat16 [1024], P('mp'), may hold values from -0.1875 to 0.1875
- texts: bfloat16 [1024, 1024], P('dp', 'mp'), may hold values from -6 to 6
- logit_scale: float32 [1], replicated, may hold values from 20 to 100
- logit_bias: float32 [1], replicated, may hold values from -4 to -1
Outputs:
- grad_pooled: bfloat16 [1024, 1024], P('dp', 'mp')
- grad_text: bfloat16 [1024, 1024], P('dp', 'mp')
The draws below stay inside these ranges and needn't reach their ends.
Inputs may be any that keep to these rules, and one draw needn't show every extreme that they name: `view_study`: study s is owned by dp index s // 16. Every study has 1 to 6 views, and some study has exactly 6. The slots of one dp index hold at most 2 views of one owner's studies, a bound reached in every draw; the views of one owner are spread over the dp indices as evenly as their number allows, and one owner holds at most 96 views, reached in every draw.
All inputs are finite; a program needn't handle non-finite values.
Results may differ from the reference program's by a relative error of at most 0.015.
Values may be sent and summed in bfloat16 or wider, within the bound.
A program may use at most 64 MiB of HBM per device.

```python
import math
import jax
import jax.numpy as jnp
from jax import lax

EMBED_WIDTH = 1024
STU_DEV = 16
CAP = 2
STUDY_COUNT = 1024
VIEWS = 8192
N_DP = 64


def draw_view_study(key, part):
    key = jax.random.fold_in(key, 7)
    key_high, key_heavy, key_counts, key_offset, key_order = jax.random.split(key, 5)
    owners = N_DP
    highest = jax.random.randint(key_high, (owners,), 2, 7)
    heavy = jax.random.randint(key_heavy, (), 0, owners)
    counts = jax.random.randint(key_counts, (owners, STU_DEV), 1, highest[:, None] + 1)
    counts = jnp.where(jnp.arange(owners)[:, None] == heavy, 6, counts)
    ends = jnp.cumsum(counts, axis=1)
    totals = ends[:, -1]
    offsets = jax.random.randint(key_offset, (owners,), 0, owners)
    sender = jnp.arange(owners)[:, None, None]
    owner = jnp.arange(owners)[None, :, None]
    slot = jnp.arange(CAP)[None, None, :]
    ranks = (sender - offsets[None, :, None]) % owners + owners * slot
    live = ranks < totals[None, :, None]
    local_study = jnp.sum((ends[None, :, None, :] <= ranks[..., None]).astype(jnp.int32), axis=-1)
    ids = jnp.where(live, owner * STU_DEV + local_study, -1)
    flat = ids.reshape(owners, owners * CAP)
    orders = jax.vmap(lambda sub: jax.random.permutation(sub, owners * CAP))(jax.random.split(key_order, owners))
    mixed = jnp.take_along_axis(flat, orders, axis=1)
    return mixed.reshape(-1).astype(jnp.int32)


def level_of(rng, dims, cuts, smallest, high):
    factor_of = 1.0
    for dim, blocks in cuts:
        steps = jax.random.uniform(jax.random.fold_in(jax.random.fold_in(rng, 6), dim), (blocks,), jnp.float32, smallest / len(cuts), high / len(cuts))
        factor_of = factor_of * jnp.repeat(jnp.exp(steps), dims[dim] // blocks).reshape((-1,) + (1,) * (len(dims) - 1 - dim))
    return factor_of


def centred(own_key, shape, width, bound, cuts=(), kind=jnp.bfloat16):
    array = width * jax.random.normal(own_key, shape, jnp.float32)
    if cuts:
        array = array * level_of(own_key, shape, cuts, -0.22, 0.18)
    return jnp.clip(array, -bound, bound).astype(kind)


def setup_inputs(seed: int = 0) -> dict:
    splits = jax.random.split(jax.random.key(seed), 7)
    views = centred(splits[0], (VIEWS, EMBED_WIDTH), 1.0, 6.0, ((0, 64), (1, 2)))
    view_study = draw_view_study(jax.random.fold_in(splits[6], 71), 0)
    pool_query = centred(splits[2], (EMBED_WIDTH,), EMBED_WIDTH ** -0.5, 0.1875, ((0, 2),))
    texts = centred(splits[3], (STUDY_COUNT, EMBED_WIDTH), 1.0, 6.0, ((0, 64), (1, 2)))
    logit_scale = jnp.clip(jnp.exp(jax.random.uniform(splits[4], (1,), jnp.float32, math.log(20.0), math.log(100.0))), 20.0, 100.0)
    logit_bias = jnp.clip(jax.random.uniform(splits[5], (1,), jnp.float32, -4.0, -1.0), -4.0, -1.0)
    return {"views": views, "view_study": view_study, "pool_query": pool_query, "texts": texts, "logit_scale": logit_scale, "logit_bias": logit_bias}


def unit_length_rescale(values):
    total = lax.optimization_barrier(jnp.sum(values * values, axis=1))
    return values * lax.rsqrt(total + 1e-06)[:, None]

def pool_views(views, view_study, pool_query):
    scores = jnp.dot(views, pool_query, preferred_element_type=jnp.float32)
    weights = jax.nn.sigmoid(scores).astype(jnp.bfloat16)
    valid = view_study >= 0
    target_labels = jnp.where(valid, view_study, 0).astype(jnp.int32)
    retained_rows = jnp.where(valid, weights.astype(jnp.float32), jnp.float32(0.0))
    weighted_views = retained_rows[:, None] * views.astype(jnp.float32)
    numerator = jax.ops.segment_sum(weighted_views, target_labels, num_segments=STUDY_COUNT)
    denominator = jax.ops.segment_sum(retained_rows, target_labels, num_segments=STUDY_COUNT)
    return numerator / denominator[:, None]

def reference(views, view_study, pool_query, texts, logit_scale, logit_bias):
    pooled = pool_views(views, view_study, pool_query)
    study_emb = unit_length_rescale(pooled).astype(jnp.bfloat16)
    report_emb = unit_length_rescale(texts.astype(jnp.float32)).astype(jnp.bfloat16)
    scale_value = logit_scale[0]
    bias_value = logit_bias[0]
    blocks = study_emb.reshape(N_DP, STU_DEV, EMBED_WIDTH)
    column_ids = jnp.arange(STUDY_COUNT).astype(jnp.int32)

    def one_block(carry, item):
        line_positions, index = item
        logits = scale_value * jnp.dot(line_positions, report_emb.T, preferred_element_type=jnp.float32) + bias_value
        own = (index * STU_DEV + jnp.arange(STU_DEV).astype(jnp.int32))[:, None] == column_ids[None, :]
        slope = (jax.nn.sigmoid(logits) - own.astype(jnp.float32)).astype(jnp.bfloat16)
        block_grad = jnp.dot(slope, report_emb, preferred_element_type=jnp.float32).astype(jnp.bfloat16)
        carry = carry + jnp.dot(slope.T, line_positions, preferred_element_type=jnp.float32)
        return (carry, block_grad)
    start_offset = jnp.zeros((STUDY_COUNT, EMBED_WIDTH), jnp.float32)
    text_gradient_total, pooled_gradients = lax.scan(one_block, start_offset, (blocks, jnp.arange(N_DP).astype(jnp.int32)))
    return (pooled_gradients.reshape(STUDY_COUNT, EMBED_WIDTH), text_gradient_total.astype(jnp.bfloat16))
```

```python
import jax
import jax.numpy as jnp
from jax import lax
from jax.experimental import pallas as pl
from jax.experimental.pallas import tpu as pltpu
from jax.sharding import PartitionSpec as P

MESH = pl.DeviceIdType.MESH
BF, F32 = jnp.bfloat16, jnp.float32
POS, LANES, HALVES = 16, 4, 2
OWN = 16
WIDTH = 512
SLOTS = 8
COL = LANES * OWN
BLK = 8
REP = BLK * OWN
CHUNK = 64
WIDE = WIDTH + 128


def nt(a, b):
    return lax.dot_general(a, b, (((1,), (1,)), ((), ())), preferred_element_type=F32)


def tn(a, b):
    return lax.dot_general(a, b, (((0,), (0,)), ((), ())), preferred_element_type=F32)


def kernel(
    views, study, query, texts, scale, bias, out_pooled, out_text,
    send_v, land_v, send_m, land_m, land_x, part, land_sib, col_sum, land_sum,
    text_part, pooled_part, land_t, land_p, ssem, rsem,
):
    dp, half = lax.axis_index("dp"), lax.axis_index("mp")
    pos, lane = dp // LANES, lax.rem(dp, LANES)
    zlo, core = lane // 2, lax.rem(lane, 2)
    other = 1 - half
    sel = lax.rem(pos, 2)
    selfish = sel == half

    barrier = pltpu.get_barrier_semaphore()

    def greet(p, l, h):
        pl.semaphore_signal(barrier, inc=1, device_id=(p * LANES + l, h), device_id_type=MESH)

    def greet_far(k, carry):
        greet(lax.rem(pos + k, POS), lane, other)
        return carry

    def greet_near(k, carry):
        greet(lax.rem(pos + k, POS), lane, half)
        return carry

    lax.fori_loop(0, POS, greet_far, 0)
    lax.fori_loop(1, POS, greet_near, 0)
    for k in range(1, LANES):
        for h in (half, other):
            greet(pos, lax.rem(lane + k, LANES), h)

    slots = views.shape[0]
    row = lax.broadcasted_iota(jnp.int32, (slots, slots), 0)
    colm = lax.broadcasted_iota(jnp.int32, (slots, slots), 1)
    ids = study[...]
    mine = (ids >> 4) == (row >> 1)
    before = (row < colm).astype(F32).astype(BF)
    hot = mine.astype(F32).astype(BF)
    rank = jnp.dot(hot, before, preferred_element_type=F32)
    pick = jnp.where(mine & (rank == (row & 1).astype(F32)), 1.0, 0.0).astype(BF)
    packed = jnp.dot(pick, views[...], preferred_element_type=F32)
    marks = jnp.broadcast_to(((ids & (COL - 1)) + 1).astype(F32), (slots, slots)).astype(BF)
    mark = nt(pick, marks)
    score = nt(packed.astype(BF), jnp.broadcast_to(query[...].astype(F32), (128, WIDTH)).astype(BF))
    high = score.astype(BF).astype(F32)
    mid = (score - high).astype(BF).astype(F32)
    low = score - high - mid
    parts = [packed[:, q * 128 : (q + 1) * 128] for q in range(4)] + [mark, high, mid, low]
    chunks = jnp.concatenate([x.reshape(POS, 1, SLOTS, 128) for x in parts], axis=1)
    send_v[...] = chunks.reshape(POS * CHUNK, 128).astype(BF)
    send_m[...] = score
    mine_rows = pl.ds(pl.multiple_of(pos * CHUNK, CHUNK), CHUNK)
    land_v[mine_rows] = send_v[mine_rows]

    pl.semaphore_wait(barrier, 2 * POS - 1 + 6)

    def copy(src, dst, i, p, l, h):
        return pltpu.make_async_remote_copy(
            src_ref=src, dst_ref=dst, send_sem=ssem.at[i], recv_sem=rsem.at[i],
            device_id=(p * LANES + l, h), device_id_type=MESH,
        )

    def done(ref, sem):
        pltpu.make_async_copy(ref, ref, sem).wait()

    def send_far(k, carry):
        p = lax.rem(pos + k, POS)
        copy(
            send_m.at[pl.ds(pl.multiple_of(p * SLOTS, SLOTS), SLOTS)],
            land_m.at[pl.ds(pl.multiple_of(pos * SLOTS, SLOTS), SLOTS)], 1, p, lane, other,
        ).start()
        return carry

    def send_near(k, carry):
        p = lax.rem(pos + k, POS)
        copy(
            send_v.at[pl.ds(pl.multiple_of(p * CHUNK, CHUNK), CHUNK)],
            land_v.at[mine_rows], 0, p, lane, half,
        ).start()
        return carry

    lax.fori_loop(0, POS, send_far, 0)
    lax.fori_loop(1, POS, send_near, 0)

    text_rows = pl.ds(pl.multiple_of((pos // 2) * OWN, OWN), OWN)

    def send_text(k, carry):
        p = lax.rem(pos + k, POS)
        copy(texts, land_x.at[half, text_rows], 2, p, lane, sel).start()
        return carry

    lax.fori_loop(1, POS, send_text, 0)

    @pl.when(selfish)
    def _():
        land_x[half, text_rows] = texts[...]

    @pl.when(jnp.logical_not(selfish))
    def _():
        copy(texts, land_x.at[half, text_rows], 2, pos, lane, sel).start()

    def done_but_self(ref, rows, sem):
        @pl.when(selfish)
        def _():
            done(ref.at[pl.ds(0, rows - OWN)], sem)

        @pl.when(jnp.logical_not(selfish))
        def _():
            done(ref, sem)

    done(land_m, rsem.at[1])
    done(land_v.at[pl.ds(0, (POS - 1) * CHUNK)], rsem.at[0])
    got = land_v[...].astype(F32).reshape(POS, 8, SLOTS, 128)
    got = [got[:, q].reshape(slots, 128) for q in range(8)]
    total = (got[5] + got[6] + got[7]) + land_m[...]
    weight = jax.nn.sigmoid(total).astype(BF).astype(F32)
    table = jnp.where(got[4] == (colm + 1).astype(F32), weight, 0.0).astype(BF)[:, :COL]
    wide = jnp.concatenate([x.astype(BF) for x in got[:4]] + [jnp.ones((slots, 128), BF)], axis=1)
    sums = tn(table, wide)
    part[...] = sums.astype(BF)
    sib = copy(part, land_sib, 3, pos, lane + 1 - 2 * core, half)
    sib.start()
    sib.wait_recv()
    col_sum[...] = (sums + land_sib[...].astype(F32)).astype(BF)
    z = half * 2 + zlo
    for k in range(1, 4):
        there = lax.rem(z + k, 4)
        copy(col_sum, land_sum.at[z], 4, pos, lax.rem(there, 2) * 2 + core, there // 2).start()
    land_sum[z] = col_sum[...]

    done_but_self(land_x.reshape(2 * REP, WIDTH), 2 * REP, rsem.at[2])
    raw = [land_x[0].astype(F32), land_x[1].astype(F32)]
    norm = jnp.sum(raw[0] * raw[0] + raw[1] * raw[1], axis=1, keepdims=True)
    inv = lax.rsqrt(norm + 1e-06)
    report = jnp.concatenate([(x * inv).astype(BF) for x in raw], axis=1)

    done(land_sum.at[pl.ds(0, 3)], rsem.at[4])
    both = [
        land_sum[2 * h].astype(F32) + land_sum[2 * h + 1].astype(F32) for h in range(HALVES)
    ]
    mean = [x[:, :WIDTH] / x[:, WIDTH : WIDTH + 1] for x in both]
    norm = jnp.sum(mean[0] * mean[0] + mean[1] * mean[1], axis=1, keepdims=True)
    inv = lax.rsqrt(norm + 1e-06)
    unit = jnp.concatenate([(x * inv).astype(BF) for x in mean], axis=1)

    logits = scale[0] * nt(unit, report) + bias[0]
    i = lax.broadcasted_iota(jnp.int32, (COL, REP), 0)
    j = lax.broadcasted_iota(jnp.int32, (COL, REP), 1)
    study_id = pos * COL + i
    report_id = ((2 * (j // OWN) + half) * LANES + lane) * OWN + lax.rem(j, OWN)
    own = (study_id == report_id).astype(F32)
    slope = (jax.nn.sigmoid(logits) - own).astype(BF)

    gt = tn(slope, unit).astype(BF)
    for h in range(HALVES):
        text_part[h] = gt[:, h * WIDTH : (h + 1) * WIDTH]

    def give_text(k, carry):
        b = lax.rem(pos // 2 + k // 2, BLK)
        h = lax.rem(half + k, 2)
        rows = pl.ds(pl.multiple_of(b * OWN, OWN), OWN)
        copy(text_part.at[h, rows], land_t.at[pos], 5, 2 * b + half, lane, h).start()
        return carry

    lax.fori_loop(1, 2 * BLK, give_text, 0)
    own_rows = pl.ds(pl.multiple_of((pos // 2) * OWN, OWN), OWN)

    @pl.when(selfish)
    def _():
        land_t[pos] = text_part[half, own_rows]

    @pl.when(jnp.logical_not(selfish))
    def _():
        b = pos // 2
        copy(text_part.at[half, own_rows], land_t.at[pos], 5, 2 * b + half, lane, half).start()

    gp = jnp.dot(slope, report, preferred_element_type=F32).astype(BF)
    for h in range(HALVES):
        pooled_part[h] = gp[:, h * WIDTH : (h + 1) * WIDTH]
    me = lane * 2 + half

    def give_pooled(k, carry):
        there = lax.rem(me + k, 8)
        l, h = there // 2, lax.rem(there, 2)
        rows = pl.ds(pl.multiple_of(l * OWN, OWN), OWN)
        copy(pooled_part.at[h, rows], land_p.at[me], 6, pos, l, h).start()
        return carry

    lax.fori_loop(1, 8, give_pooled, 0)
    land_p[me] = pooled_part[half, pl.ds(pl.multiple_of(lane * OWN, OWN), OWN)]

    done(land_p.at[pl.ds(0, 7)], rsem.at[6])
    out_pooled[...] = jnp.sum(land_p[...].astype(F32), axis=0).astype(BF)
    done_but_self(land_t.reshape(POS * OWN, WIDTH), POS * OWN, rsem.at[5])
    out_text[...] = jnp.sum(land_t[...].astype(F32), axis=0).astype(BF)

    done(send_v.at[pl.ds(0, (POS - 1) * CHUNK)], ssem.at[0])
    done(send_m, ssem.at[1])
    done_but_self(land_x.reshape(2 * REP, WIDTH), 2 * REP, ssem.at[2])
    sib.wait_send()
    done(land_sum.at[pl.ds(0, 3)], ssem.at[4])
    done_but_self(land_t.reshape(POS * OWN, WIDTH), POS * OWN, ssem.at[5])
    done(land_p.at[pl.ds(0, 7)], ssem.at[6])


def on_device(views, view_study, pool_query, texts, logit_scale, logit_bias):
    slots = views.shape[0]
    vmem = pl.BlockSpec(memory_space=pltpu.VMEM)
    smem = pl.BlockSpec(memory_space=pltpu.SMEM)
    out = jax.ShapeDtypeStruct((OWN, WIDTH), BF)
    return pl.pallas_call(
        kernel,
        out_shape=(out, out),
        in_specs=[vmem, vmem, vmem, vmem, smem, smem],
        out_specs=(vmem, vmem),
        scratch_shapes=[
            pltpu.VMEM((POS * CHUNK, 128), BF),
            pltpu.VMEM((POS * CHUNK, 128), BF),
            pltpu.VMEM((slots, 128), F32),
            pltpu.VMEM((slots, 128), F32),
            pltpu.VMEM((HALVES, REP, WIDTH), BF),
            pltpu.VMEM((COL, WIDE), BF),
            pltpu.VMEM((COL, WIDE), BF),
            pltpu.VMEM((COL, WIDE), BF),
            pltpu.VMEM((4, COL, WIDE), BF),
            pltpu.VMEM((HALVES, REP, WIDTH), BF),
            pltpu.VMEM((HALVES, COL, WIDTH), BF),
            pltpu.VMEM((POS, OWN, WIDTH), BF),
            pltpu.VMEM((LANES * HALVES, OWN, WIDTH), BF),
            pltpu.SemaphoreType.DMA((7,)),
            pltpu.SemaphoreType.DMA((7,)),
        ],
        compiler_params=pltpu.CompilerParams(
            collective_id=0, has_side_effects=True, vmem_limit_bytes=32 << 20
        ),
    )(
        views, view_study.reshape(1, slots), pool_query.reshape(1, WIDTH), texts,
        logit_scale, logit_bias,
    )


def solution(mesh):
    in_specs = (P("dp", "mp"), P("dp"), P("mp"), P("dp", "mp"), P(), P())
    out_specs = (P("dp", "mp"), P("dp", "mp"))
    return jax.shard_map(
        on_device, mesh=mesh, in_specs=in_specs, out_specs=out_specs, check_vma=False
    )
```

```python
import jax
import jax.numpy as jnp
from jax import lax
from jax.experimental import pallas as pl
from jax.experimental.pallas import tpu as pltpu
from jax.sharding import PartitionSpec as P

MESH = pl.DeviceIdType.MESH
BF, F32 = jnp.bfloat16, jnp.float32
SIDE = 4
POS, LANES, HALVES = 16, 4, 2
OWN = 16
WIDTH = 512
SLOTS = 8
COL = LANES * OWN
BLK = 8
REP = BLK * OWN
CHUNK = 48
WIDE = WIDTH + 128

NEAR = {0: 0, 1: 1, 2: 2, 3: 1}
STEPS = sorted(
    ((dy, dx) for dy in range(SIDE) for dx in range(SIDE)), key=lambda s: -NEAR[s[0]] - NEAR[s[1]]
)


def nt(a, b):
    return lax.dot_general(a, b, (((1,), (1,)), ((), ())), preferred_element_type=F32)


def tn(a, b):
    return lax.dot_general(a, b, (((0,), (0,)), ((), ())), preferred_element_type=F32)


def kernel(
    views_in, study_in, query_in, texts_in, scale, bias, out_pooled, out_text,
    views, study, query, texts, send_v, land_v, send_s, land_s, land_x, part, land_sib, col_sum, land_sum,
    text_part, pooled_part, land_t, land_p, ssem, rsem, lsem,
):
    dp, half = lax.axis_index("dp"), lax.axis_index("mp")
    pos, lane = dp // LANES, lax.rem(dp, LANES)
    py, px = pos // SIDE, lax.rem(pos, SIDE)
    zlo, core = lane // 2, lax.rem(lane, 2)
    other = 1 - half
    cross = (1 - zlo) * 2 + core

    def at(dy, dx):
        return lax.rem(py + dy, SIDE) * SIDE + lax.rem(px + dx, SIDE)

    barrier = pltpu.get_barrier_semaphore()

    def greet(p, l, h):
        pl.semaphore_signal(barrier, inc=1, device_id=(p * LANES + l, h), device_id_type=MESH)

    for dy, dx in STEPS[:-1]:
        greet(at(dy, dx), lane, half)
    greet(pos, lane, other)
    for k in range(1, LANES):
        for h in (other, half):
            greet(pos, lax.rem(lane + k, LANES), h)

    loads = [
        pltpu.make_async_copy(a, b, lsem.at[i])
        for i, (a, b) in enumerate(
            [(study_in, study), (views_in, views), (query_in, query), (texts_in, texts)]
        )
    ]
    for load in loads:
        load.start()
    drains = []

    for load in loads:
        load.wait()

    slots = views.shape[0]
    row = lax.broadcasted_iota(jnp.int32, (slots, slots), 0)
    colm = lax.broadcasted_iota(jnp.int32, (slots, slots), 1)
    ids = study[...]
    mine = (ids >> 4) == (row >> 1)
    before = (row < colm).astype(F32).astype(BF)
    hot = mine.astype(F32).astype(BF)
    rank = jnp.dot(hot, before, preferred_element_type=F32)
    pick = jnp.where(mine & (rank == (row & 1).astype(F32)), 1.0, 0.0).astype(BF)
    packed = jnp.dot(pick, views[...], preferred_element_type=F32)
    marks = jnp.broadcast_to(((ids & (COL - 1)) + 1).astype(F32), (slots, slots)).astype(BF)
    mark = nt(pick, marks)
    parts = [packed[:, q * 128 : (q + 1) * 128] for q in range(4)] + [mark, mark]
    chunks = jnp.concatenate([x.reshape(POS, 1, SLOTS, 128) for x in parts], axis=1)
    send_v[...] = chunks.reshape(POS * CHUNK, 128).astype(BF)
    mine_rows = pl.ds(pl.multiple_of(pos * CHUNK, CHUNK), CHUNK)
    land_v[mine_rows] = send_v[mine_rows]
    ask = jnp.broadcast_to(query[...].reshape(1, WIDTH).astype(F32), (SLOTS, WIDTH)).astype(BF)

    pl.semaphore_wait(barrier, POS - 1 + 7)

    def copy(src, dst, i, p, l, h):
        return pltpu.make_async_remote_copy(
            src_ref=src, dst_ref=dst, send_sem=ssem.at[i], recv_sem=rsem.at[i],
            device_id=(p * LANES + l, h), device_id_type=MESH,
        )

    def done(ref, sem):
        pltpu.make_async_copy(ref, ref, sem).wait()

    for dy, dx in STEPS[:-1]:
        p = at(dy, dx)
        copy(
            send_v.at[pl.ds(pl.multiple_of(p * CHUNK, CHUNK), CHUNK)],
            land_v.at[mine_rows], 0, p, lane, half,
        ).start()
    drains.append(lambda: done(send_v.at[pl.ds(0, (POS - 1) * CHUNK)], ssem.at[0]))

    done(land_v.at[pl.ds(0, (POS - 1) * CHUNK)], rsem.at[0])
    got = land_v[...].astype(F32).reshape(POS, CHUNK // SLOTS, SLOTS, 128)
    got = [got[:, q].reshape(slots, 128).astype(BF) for q in range(5)]
    held = jnp.concatenate(got[:4], axis=1)
    score = nt(ask, held)
    send_s[...] = score
    swap = copy(send_s, land_s, 1, pos, lane, other)
    swap.start()
    drains.append(swap.wait_send)

    text_rows = pl.ds(pl.multiple_of((pos // 2) * OWN, OWN), OWN)
    sel = lax.rem(pos, 2)
    for dy, dx in STEPS:
        copy(texts, land_x.at[half, text_rows], 2, at(dy, dx), cross, sel).start()
    drains.append(lambda: done(land_x, ssem.at[2]))

    mark_row = nt(jnp.where(colm[:SLOTS] == 0, 1.0, 0.0).astype(BF), got[4])[:1]
    swap.wait_recv()
    weight = jax.nn.sigmoid(score + land_s[...]).astype(BF).astype(F32)[:1]
    table = jnp.where(mark_row == (row[:COL] + 1).astype(F32), weight, 0.0).astype(BF)
    wide = jnp.concatenate([held, jnp.ones((slots, 128), BF)], axis=1)
    sums = jnp.dot(table, wide, preferred_element_type=F32)
    part[...] = sums.astype(BF)
    sib = copy(part, land_sib, 3, pos, lane + 1 - 2 * core, half)
    sib.start()
    sib.wait_recv()
    drains.append(sib.wait_send)
    col_sum[...] = (sums + land_sib[...].astype(F32)).astype(BF)
    z = half * 2 + zlo
    for k in (2, 1, 3):
        there = lax.rem(z + k, 4)
        copy(col_sum, land_sum.at[z], 4, pos, lax.rem(there, 2) * 2 + core, there // 2).start()
    land_sum[z] = col_sum[...]
    drains.append(lambda: done(land_sum.at[pl.ds(0, 3)], ssem.at[4]))

    done(land_x, rsem.at[2])
    raw = [land_x[0].astype(F32), land_x[1].astype(F32)]
    norm = jnp.sum(raw[0] * raw[0] + raw[1] * raw[1], axis=1, keepdims=True)
    inv = lax.rsqrt(norm + 1e-06)
    report = jnp.concatenate([(x * inv).astype(BF) for x in raw], axis=1)

    done(land_sum.at[pl.ds(0, 3)], rsem.at[4])
    both = [
        land_sum[2 * h].astype(F32) + land_sum[2 * h + 1].astype(F32) for h in range(HALVES)
    ]
    mean = [x[:, :WIDTH] / x[:, WIDTH : WIDTH + 1] for x in both]
    norm = jnp.sum(mean[0] * mean[0] + mean[1] * mean[1], axis=1, keepdims=True)
    inv = lax.rsqrt(norm + 1e-06)
    unit = jnp.concatenate([(x * inv).astype(BF) for x in mean], axis=1)

    logits = scale[0] * nt(unit, report) + bias[0]
    i = lax.broadcasted_iota(jnp.int32, (COL, REP), 0)
    j = lax.broadcasted_iota(jnp.int32, (COL, REP), 1)
    study_id = pos * COL + i
    report_id = ((2 * (j // OWN) + half) * LANES + cross) * OWN + lax.rem(j, OWN)
    own = (study_id == report_id).astype(F32)
    slope = (jax.nn.sigmoid(logits) - own).astype(BF)

    gt = tn(slope, unit).astype(BF)
    for h in range(HALVES):
        text_part[h] = gt[:, h * WIDTH : (h + 1) * WIDTH]
    odd = lax.rem(px + half, 2)
    for dy in (2, 1, 3, 0):
        for dx in (2, 0):
            p = at(dy, dx + odd)
            rows = pl.ds(pl.multiple_of((p // 2) * OWN, OWN), OWN)
            for h in range(HALVES):
                copy(text_part.at[h, rows], land_t.at[pos], 5, p, cross, h).start()
    drains.append(lambda: done(land_t, ssem.at[5]))

    gp = jnp.dot(slope, report, preferred_element_type=F32).astype(BF)
    for h in range(HALVES):
        pooled_part[h] = gp[:, h * WIDTH : (h + 1) * WIDTH]
    me = lane * 2 + half
    for k in range(1, 8):
        there = lax.rem(me + k, 8)
        l, h = there // 2, lax.rem(there, 2)
        rows = pl.ds(pl.multiple_of(l * OWN, OWN), OWN)
        copy(pooled_part.at[h, rows], land_p.at[me], 6, pos, l, h).start()
    land_p[me] = pooled_part[half, pl.ds(pl.multiple_of(lane * OWN, OWN), OWN)]
    drains.append(lambda: done(land_p.at[pl.ds(0, 7)], ssem.at[6]))

    done(land_p.at[pl.ds(0, 7)], rsem.at[6])
    out_pooled[...] = jnp.sum(land_p[...].astype(F32), axis=0).astype(BF)
    done(land_t, rsem.at[5])
    out_text[...] = jnp.sum(land_t[...].astype(F32), axis=0).astype(BF)
    for drain in drains:
        drain()


def on_device(views, view_study, pool_query, texts, logit_scale, logit_bias):
    slots = views.shape[0]
    vmem = pl.BlockSpec(memory_space=pltpu.VMEM)
    hbm = pl.BlockSpec(memory_space=pltpu.HBM)
    smem = pl.BlockSpec(memory_space=pltpu.SMEM)
    out = jax.ShapeDtypeStruct((OWN, WIDTH), BF)
    return pl.pallas_call(
        kernel,
        out_shape=(out, out),
        in_specs=[hbm, hbm, hbm, hbm, smem, smem],
        out_specs=(vmem, vmem),
        scratch_shapes=[
            pltpu.VMEM((slots, WIDTH), BF),
            pltpu.VMEM((1, slots), jnp.int32),
            pltpu.VMEM((WIDTH,), BF),
            pltpu.VMEM((OWN, WIDTH), BF),
            pltpu.VMEM((POS * CHUNK, 128), BF),
            pltpu.VMEM((POS * CHUNK, 128), BF),
            pltpu.VMEM((SLOTS, 128), F32),
            pltpu.VMEM((SLOTS, 128), F32),
            pltpu.VMEM((HALVES, REP, WIDTH), BF),
            pltpu.VMEM((COL, WIDE), BF),
            pltpu.VMEM((COL, WIDE), BF),
            pltpu.VMEM((COL, WIDE), BF),
            pltpu.VMEM((4, COL, WIDE), BF),
            pltpu.VMEM((HALVES, REP, WIDTH), BF),
            pltpu.VMEM((HALVES, COL, WIDTH), BF),
            pltpu.VMEM((POS, OWN, WIDTH), BF),
            pltpu.VMEM((LANES * HALVES, OWN, WIDTH), BF),
            pltpu.SemaphoreType.DMA((7,)),
            pltpu.SemaphoreType.DMA((7,)),
            pltpu.SemaphoreType.DMA((4,)),
        ],
        compiler_params=pltpu.CompilerParams(
            collective_id=0, has_side_effects=True, vmem_limit_bytes=63 << 20
        ),
    )(
        views, view_study.reshape(1, slots), pool_query, texts,
        logit_scale, logit_bias,
    )


def solution(mesh):
    in_specs = (P("dp", "mp"), P("dp"), P("mp"), P("dp", "mp"), P(), P())
    out_specs = (P("dp", "mp"), P("dp", "mp"))
    return jax.shard_map(
        on_device, mesh=mesh, in_specs=in_specs, out_specs=out_specs, check_vma=False
    )
```

```python
import jax
import jax.numpy as jnp
from jax import lax
from jax.experimental import pallas as pl
from jax.experimental.pallas import tpu as pltpu
from jax.sharding import PartitionSpec as P

MESH = pl.DeviceIdType.MESH
BF, F32 = jnp.bfloat16, jnp.float32
SIDE = 4
POS, LANES, HALVES = 16, 4, 2
OWN = 16
WIDTH = 512
SLOTS = 8
COL = LANES * OWN
BLK = 8
REP = BLK * OWN
CHUNK = 32
WIDE = WIDTH + 128

NEAR = {0: 0, 1: 1, 2: 2, 3: 1}
STEPS = sorted(
    ((dy, dx) for dy in range(SIDE) for dx in range(SIDE)), key=lambda s: -NEAR[s[0]] - NEAR[s[1]]
)


def nt(a, b):
    return lax.dot_general(a, b, (((1,), (1,)), ((), ())), preferred_element_type=F32)


def tn(a, b):
    return lax.dot_general(a, b, (((0,), (0,)), ((), ())), preferred_element_type=F32)


def kernel(
    views_in, study_in, query_in, texts_in, scale, bias, out_pooled, out_text,
    views, study, query, texts, send_v, land_v, send_s, land_s, land_r, land_x, part, land_sib, col_sum, land_sum,
    land_den, text_part, pooled_part, land_t, land_p, ssem, rsem, lsem,
):
    dp, half = lax.axis_index("dp"), lax.axis_index("mp")
    pos, lane = dp // LANES, lax.rem(dp, LANES)
    py, px = pos // SIDE, lax.rem(pos, SIDE)
    zlo, core = lane // 2, lax.rem(lane, 2)
    other = 1 - half
    cross = (1 - zlo) * 2 + core

    def at(dy, dx):
        return lax.rem(py + dy, SIDE) * SIDE + lax.rem(px + dx, SIDE)

    barrier = pltpu.get_barrier_semaphore()

    def greet(p, l, h):
        pl.semaphore_signal(barrier, inc=1, device_id=(p * LANES + l, h), device_id_type=MESH)

    for dy, dx in STEPS:
        greet(at(dy, dx), lane, other)
    for dy, dx in STEPS[:-1]:
        greet(at(dy, dx), lane, half)
    for k in range(1, LANES):
        for h in (other, half):
            greet(pos, lax.rem(lane + k, LANES), h)

    loads = [
        pltpu.make_async_copy(a, b, lsem.at[i])
        for i, (a, b) in enumerate(
            [(study_in, study), (views_in, views), (query_in, query), (texts_in, texts)]
        )
    ]
    for load in loads:
        load.start()
    drains = []

    for load in loads:
        load.wait()

    slots = views.shape[0]
    row = lax.broadcasted_iota(jnp.int32, (slots, slots), 0)
    colm = lax.broadcasted_iota(jnp.int32, (slots, slots), 1)
    ids = study[...]
    mine = (ids >> 4) == (row >> 1)
    before = (row < colm).astype(F32).astype(BF)
    hot = mine.astype(F32).astype(BF)
    rank = jnp.dot(hot, before, preferred_element_type=F32)
    pick = jnp.where(mine & (rank == (row & 1).astype(F32)), 1.0, 0.0).astype(BF)
    packed = jnp.dot(pick, views[...], preferred_element_type=F32)
    marks = jnp.broadcast_to(((ids & (COL - 1)) + 1).astype(F32), (slots, slots)).astype(BF)
    mark = nt(pick, marks)
    ask = jnp.broadcast_to(query[...].reshape(1, WIDTH).astype(F32), (slots, WIDTH)).astype(BF)
    score = nt(packed.astype(BF), ask)
    place = colm == pos * SLOTS + (row & (SLOTS - 1))
    for k, x in enumerate((score, mark)):
        send_s[:, k, :] = jnp.sum(jnp.where(place, x, 0.0).reshape(POS, SLOTS, 128), axis=1)
    parts = [packed[:, q * 128 : (q + 1) * 128] for q in range(4)]
    chunks = jnp.concatenate([x.reshape(POS, 1, SLOTS, 128) for x in parts], axis=1)
    send_v[...] = chunks.reshape(POS * CHUNK, 128).astype(BF)
    mine_rows = pl.ds(pl.multiple_of(pos * CHUNK, CHUNK), CHUNK)
    land_v[mine_rows] = send_v[mine_rows]
    pl.semaphore_wait(barrier, 2 * POS - 1 + 6)

    def copy(src, dst, i, p, l, h):
        return pltpu.make_async_remote_copy(
            src_ref=src, dst_ref=dst, send_sem=ssem.at[i], recv_sem=rsem.at[i],
            device_id=(p * LANES + l, h), device_id_type=MESH,
        )

    def done(ref, sem):
        pltpu.make_async_copy(ref, ref, sem).wait()

    sel = lax.rem(pos + core, 2)
    giver = sel == half
    copy(texts, land_r.at[half], 8, pos, cross, sel).start()
    drains.append(lambda: done(texts, ssem.at[8]))
    for dy, dx in STEPS[:-1]:
        p = at(dy, dx)
        copy(
            send_v.at[pl.ds(pl.multiple_of(p * CHUNK, CHUNK), CHUNK)],
            land_v.at[mine_rows], 0, p, lane, half,
        ).start()
    drains.append(lambda: done(send_v.at[pl.ds(0, (POS - 1) * CHUNK)], ssem.at[0]))
    for dy, dx in STEPS:
        p = at(dy, dx)
        copy(send_s.at[p], land_s.at[pos], 1, p, lane, other).start()
    drains.append(lambda: done(send_s, ssem.at[1]))

    done(land_v.at[pl.ds(0, (POS - 1) * CHUNK)], rsem.at[0])
    got = land_v[...].astype(F32).reshape(POS, CHUNK // SLOTS, SLOTS, 128)
    held = jnp.concatenate([got[:, q].reshape(slots, 128).astype(BF) for q in range(4)], axis=1)
    score = nt(ask[:SLOTS], held)[:1]


    @pl.when(giver)
    def _():
        done(land_r, rsem.at[8])
        for dy, dx in STEPS[:-1]:
            copy(land_r, land_x.at[pos // 2], 2, at(dy, dx), lane, half).start()
        land_x[pos // 2] = land_r[...]

    def handed():
        @pl.when(giver)
        def _():
            done(land_x, ssem.at[2])
            done(land_x.at[pl.ds(0, BLK - 1)], ssem.at[2])

    drains.append(handed)

    done(land_s, rsem.at[1])
    more = jnp.sum(land_s[...], axis=0)
    weight = jax.nn.sigmoid(score + more[:1]).astype(BF).astype(F32)
    table = jnp.where(more[1:] == (row[:COL] + 1).astype(F32), weight, 0.0).astype(BF)
    wide = jnp.concatenate([held, jnp.ones((slots, 128), BF)], axis=1)
    sums = jnp.dot(table, wide, preferred_element_type=F32)
    part[...] = sums.astype(BF)
    sib = copy(part, land_sib, 3, pos, lane + 1 - 2 * core, half)
    sib.start()
    sib.wait_recv()
    drains.append(sib.wait_send)
    col_sum[...] = (sums + land_sib[...].astype(F32)).astype(BF)
    z = half * 2 + zlo
    for k in (2, 1, 3):
        there = lax.rem(z + k, 4)
        copy(
            col_sum.at[:, pl.ds(0, WIDTH)], land_sum.at[z], 4, pos, lax.rem(there, 2) * 2 + core, there // 2
        ).start()
    copy(col_sum.at[:, pl.ds(WIDTH, 128)], land_den, 7, pos, cross, half).start()
    land_sum[z] = col_sum[:, :WIDTH]
    drains.append(lambda: done(land_sum.at[pl.ds(0, 3)], ssem.at[4]))
    drains.append(lambda: done(land_den, ssem.at[7]))

    @pl.when(giver)
    def _():
        done(land_x.at[pl.ds(0, BLK - 1)], rsem.at[2])

    @pl.when(jnp.logical_not(giver))
    def _():
        done(land_x, rsem.at[2])

    raw = [land_x[:, h].reshape(REP, WIDTH).astype(F32) for h in range(HALVES)]
    norm = jnp.sum(raw[0] * raw[0] + raw[1] * raw[1], axis=1, keepdims=True)
    inv = lax.rsqrt(norm + 1e-06)
    report = jnp.concatenate([(x * inv).astype(BF) for x in raw], axis=1)

    done(land_den, rsem.at[7])
    done(land_sum.at[pl.ds(0, 3)], rsem.at[4])
    both = [
        land_sum[2 * h].astype(F32) + land_sum[2 * h + 1].astype(F32) for h in range(HALVES)
    ]
    weights = col_sum[:, WIDTH:].astype(F32) + land_den[...].astype(F32)
    mean = [x / weights[:, :1] for x in both]
    norm = jnp.sum(mean[0] * mean[0] + mean[1] * mean[1], axis=1, keepdims=True)
    inv = lax.rsqrt(norm + 1e-06)
    unit = jnp.concatenate([(x * inv).astype(BF) for x in mean], axis=1)

    logits = scale[0] * nt(unit, report) + bias[0]
    i = lax.broadcasted_iota(jnp.int32, (COL, REP), 0)
    j = lax.broadcasted_iota(jnp.int32, (COL, REP), 1)
    study_id = pos * COL + i
    report_id = ((2 * (j // OWN) + lax.rem(half + core, 2)) * LANES + cross) * OWN + lax.rem(j, OWN)
    own = (study_id == report_id).astype(F32)
    slope = (jax.nn.sigmoid(logits) - own).astype(BF)

    gt = tn(slope, unit).astype(BF)
    for h in range(HALVES):
        text_part[h] = gt[:, h * WIDTH : (h + 1) * WIDTH]
    odd = lax.rem(px + half + core, 2)
    for dy in (2, 1, 3, 0):
        for dx in (2, 0):
            p = at(dy, dx + odd)
            rows = pl.ds(pl.multiple_of((p // 2) * OWN, OWN), OWN)
            for h in range(HALVES):
                copy(text_part.at[h, rows], land_t.at[pos], 5, p, cross, h).start()
    drains.append(lambda: done(land_t, ssem.at[5]))

    gp = jnp.dot(slope, report, preferred_element_type=F32).astype(BF)
    for h in range(HALVES):
        pooled_part[h] = gp[:, h * WIDTH : (h + 1) * WIDTH]
    me = lane * 2 + half
    for k in range(1, 8):
        there = lax.rem(me + k, 8)
        l, h = there // 2, lax.rem(there, 2)
        rows = pl.ds(pl.multiple_of(l * OWN, OWN), OWN)
        copy(pooled_part.at[h, rows], land_p.at[me], 6, pos, l, h).start()
    land_p[me] = pooled_part[half, pl.ds(pl.multiple_of(lane * OWN, OWN), OWN)]
    drains.append(lambda: done(land_p.at[pl.ds(0, 7)], ssem.at[6]))

    done(land_p.at[pl.ds(0, 7)], rsem.at[6])
    out_pooled[...] = jnp.sum(land_p[...].astype(F32), axis=0).astype(BF)
    done(land_t, rsem.at[5])
    out_text[...] = jnp.sum(land_t[...].astype(F32), axis=0).astype(BF)
    for drain in drains:
        drain()


def on_device(views, view_study, pool_query, texts, logit_scale, logit_bias):
    slots = views.shape[0]
    vmem = pl.BlockSpec(memory_space=pltpu.VMEM)
    hbm = pl.BlockSpec(memory_space=pltpu.HBM)
    smem = pl.BlockSpec(memory_space=pltpu.SMEM)
    out = jax.ShapeDtypeStruct((OWN, WIDTH), BF)
    return pl.pallas_call(
        kernel,
        out_shape=(out, out),
        in_specs=[hbm, hbm, hbm, hbm, smem, smem],
        out_specs=(vmem, vmem),
        scratch_shapes=[
            pltpu.VMEM((slots, WIDTH), BF),
            pltpu.VMEM((1, slots), jnp.int32),
            pltpu.VMEM((WIDTH,), BF),
            pltpu.VMEM((OWN, WIDTH), BF),
            pltpu.VMEM((POS * CHUNK, 128), BF),
            pltpu.VMEM((POS * CHUNK, 128), BF),
            pltpu.VMEM((POS, 2, 128), F32),
            pltpu.VMEM((POS, 2, 128), F32),
            pltpu.VMEM((HALVES, OWN, WIDTH), BF),
            pltpu.VMEM((BLK, HALVES, OWN, WIDTH), BF),
            pltpu.VMEM((COL, WIDE), BF),
            pltpu.VMEM((COL, WIDE), BF),
            pltpu.VMEM((COL, WIDE), BF),
            pltpu.VMEM((4, COL, WIDTH), BF),
            pltpu.VMEM((COL, 128), BF),
            pltpu.VMEM((HALVES, REP, WIDTH), BF),
            pltpu.VMEM((HALVES, COL, WIDTH), BF),
            pltpu.VMEM((POS, OWN, WIDTH), BF),
            pltpu.VMEM((LANES * HALVES, OWN, WIDTH), BF),
            pltpu.SemaphoreType.DMA((9,)),
            pltpu.SemaphoreType.DMA((9,)),
            pltpu.SemaphoreType.DMA((4,)),
        ],
        compiler_params=pltpu.CompilerParams(
            collective_id=0, has_side_effects=True, vmem_limit_bytes=32 << 20
        ),
    )(
        *(pltpu.with_memory_space_constraint(x, pltpu.HBM) for x in (views, view_study.reshape(1, slots), pool_query, texts)),
        logit_scale, logit_bias,
    )


def solution(mesh):
    in_specs = (P("dp", "mp"), P("dp"), P("mp"), P("dp", "mp"), P(), P())
    out_specs = (P("dp", "mp"), P("dp", "mp"))
    return jax.shard_map(
        on_device, mesh=mesh, in_specs=in_specs, out_specs=out_specs, check_vma=False
    )
```

```python
import jax
import jax.numpy as jnp
from jax import lax
from jax.experimental import pallas as pl
from jax.experimental.pallas import tpu as pltpu
from jax.sharding import PartitionSpec as P

MESH = pl.DeviceIdType.MESH
BF, F32 = jnp.bfloat16, jnp.float32
SIDE = 4
POS, LANES, HALVES = 16, 4, 2
OWN = 16
WIDTH = 512
SLOTS = 8
COL = LANES * OWN
BLK = 8
REP = BLK * OWN
PIECE = WIDTH // 2
CHUNK = 2 * SLOTS
WIDE = WIDTH + 128

NEAR = {0: 0, 1: 1, 2: 2, 3: 1}
STEPS = sorted(
    ((dy, dx) for dy in range(SIDE) for dx in range(SIDE)), key=lambda s: -NEAR[s[0]] - NEAR[s[1]]
)


def nt(a, b):
    return lax.dot_general(a, b, (((1,), (1,)), ((), ())), preferred_element_type=F32)


def tn(a, b):
    return lax.dot_general(a, b, (((0,), (0,)), ((), ())), preferred_element_type=F32)


def kernel(
    views_in, study_in, query_in, texts_in, scale, bias, out_pooled, out_text,
    views, study, query, texts, send_v, land_v, send_s, land_s, land_r, land_x, part, land_sib, col_sum, land_sum,
    land_den, text_part, pooled_part, land_t, land_p, ssem, rsem, lsem,
):
    dp, half = lax.axis_index("dp"), lax.axis_index("mp")
    pos, lane = dp // LANES, lax.rem(dp, LANES)
    py, px = pos // SIDE, lax.rem(pos, SIDE)
    zlo, core = lane // 2, lax.rem(lane, 2)
    other = 1 - half
    cross = (1 - zlo) * 2 + core

    def at(dy, dx):
        return lax.rem(py + dy, SIDE) * SIDE + lax.rem(px + dx, SIDE)

    loads = [
        pltpu.make_async_copy(a, b, lsem.at[i])
        for i, (a, b) in enumerate(
            [(study_in, study), (views_in, views), (query_in, query), (texts_in, texts)]
        )
    ]
    for load in loads:
        load.start()
    barrier = pltpu.get_barrier_semaphore()

    def greet(p, l, h):
        pl.semaphore_signal(barrier, inc=1, device_id=(p * LANES + l, h), device_id_type=MESH)

    for dy, dx in STEPS:
        greet(at(dy, dx), lane, other)
    for dy, dx in STEPS[:-1]:
        greet(at(dy, dx), lane, half)
    for k in range(1, LANES):
        for h in (other, half):
            greet(pos, lax.rem(lane + k, LANES), h)

    drains = []

    loads[0].wait()
    slots = views.shape[0]
    row = lax.broadcasted_iota(jnp.int32, (slots, slots), 0)
    colm = lax.broadcasted_iota(jnp.int32, (slots, slots), 1)
    ids = study[...]
    mine = (ids >> 4) == (row >> 1)
    before = (row < colm).astype(F32).astype(BF)
    hot = mine.astype(F32).astype(BF)
    rank = jnp.dot(hot, before, preferred_element_type=F32)
    chosen = mine & (rank == (row & 1).astype(F32))
    pick = chosen.astype(F32).astype(BF)
    loads[1].wait()
    packed = jnp.dot(pick, views[...], preferred_element_type=F32)
    loads[2].wait()
    asked = query[...].reshape(1, WIDTH).astype(F32)
    score = nt(jnp.broadcast_to(asked, (SLOTS, WIDTH)).astype(BF), views[...])[:1]
    mark = ((ids & (COL - 1)) + 1).astype(F32)
    wide_row = lax.broadcasted_iota(jnp.int32, (slots, POS * CHUNK), 0)
    wide_col = lax.broadcasted_iota(jnp.int32, (slots, POS * CHUNK), 1)
    place = (colm // CHUNK == lax.rem(pos, 8)) & ((colm & (SLOTS - 1)) == (row & (SLOTS - 1)))
    for k, x in enumerate((score, mark)):
        x = jnp.sum(jnp.where(chosen, x, 0.0), axis=1, keepdims=True)
        send_s[:, k, :] = jnp.sum(jnp.where(place, x, 0.0).reshape(POS, SLOTS, 128), axis=1)
    parts = [packed[:, q * PIECE : (q + 1) * PIECE] for q in range(2)]
    ask = jnp.concatenate(
        [jnp.broadcast_to(asked[:, q * PIECE : (q + 1) * PIECE], (SLOTS, PIECE)) for q in range(2)], axis=0
    ).astype(BF)
    chunks = jnp.concatenate([x.reshape(POS, 1, SLOTS, PIECE) for x in parts], axis=1)
    send_v[...] = chunks.reshape(POS * CHUNK, PIECE).astype(BF)
    mine_rows = pl.ds(pl.multiple_of(pos * CHUNK, CHUNK), CHUNK)
    land_v[mine_rows] = send_v[mine_rows]
    pl.semaphore_wait(barrier, 2 * POS - 1 + 6)

    def copy(src, dst, i, p, l, h):
        return pltpu.make_async_remote_copy(
            src_ref=src, dst_ref=dst, send_sem=ssem.at[i], recv_sem=rsem.at[i],
            device_id=(p * LANES + l, h), device_id_type=MESH,
        )

    def done(ref, sem):
        pltpu.make_async_copy(ref, ref, sem).wait()

    sel = lax.rem(pos + core, 2)
    giver = sel == half
    loads[3].wait()
    copy(texts, land_r.at[half], 8, pos, cross, sel).start()
    drains.append(lambda: done(texts, ssem.at[8]))
    for dy, dx in STEPS:
        p = at(dy, dx)
        copy(send_s.at[p], land_s.at[pos], 1, p, lane, other).start()
    for dy, dx in STEPS[:-1]:
        p = at(dy, dx)
        copy(
            send_v.at[pl.ds(pl.multiple_of(p * CHUNK, CHUNK), CHUNK)],
            land_v.at[mine_rows], 0, p, lane, half,
        ).start()
    drains.append(lambda: done(send_v.at[pl.ds(0, (POS - 1) * CHUNK)], ssem.at[0]))
    drains.append(lambda: done(send_s, ssem.at[1]))

    done(land_v.at[pl.ds(0, (POS - 1) * CHUNK)], rsem.at[0])
    held = land_v[...]
    second = (lax.broadcasted_iota(jnp.int32, (1, POS * CHUNK), 1) & SLOTS) != 0
    piece = nt(ask, held)
    piece = jnp.where(second, piece[SLOTS : SLOTS + 1], piece[:1])
    rest = jnp.where(second, pltpu.roll(piece, SLOTS, 1), pltpu.roll(piece, POS * CHUNK - SLOTS, 1))

    @pl.when(giver)
    def _():
        done(land_r, rsem.at[8])
        for dy, dx in STEPS[:-1]:
            copy(land_r, land_x.at[pos // 2], 2, at(dy, dx), lane, half).start()
        land_x[pos // 2] = land_r[...]

    def handed():
        @pl.when(giver)
        def _():
            done(land_x, ssem.at[2])
            done(land_x.at[pl.ds(0, BLK - 1)], ssem.at[2])

    drains.append(handed)

    done(land_s, rsem.at[1])
    more = jnp.sum(land_s[...].reshape(2, 8, 2, 128), axis=1)
    more = jnp.concatenate([more[0], more[1]], axis=1)
    weight = jax.nn.sigmoid(piece + rest + more[:1]).astype(BF).astype(F32)
    study_row = (wide_row & (COL - 1)) + 1
    fits = (more[1:] == study_row.astype(F32)) & (((wide_row & COL) != 0) == ((wide_col & SLOTS) != 0))
    table = jnp.where(fits, weight, 0.0).astype(BF)
    sums = jnp.dot(table, held, preferred_element_type=F32)
    total = jnp.dot(table[:COL], jnp.ones((POS * CHUNK, 128), BF), preferred_element_type=F32)
    sums = jnp.concatenate([sums[:COL], sums[COL:], total], axis=1)
    part[...] = sums.astype(BF)
    sib = copy(part, land_sib, 3, pos, lane + 1 - 2 * core, half)
    sib.start()
    sib.wait_recv()
    drains.append(sib.wait_send)
    col_sum[...] = (sums + land_sib[...].astype(F32)).astype(BF)
    z = half * 2 + zlo
    for k in (2, 1, 3):
        there = lax.rem(z + k, 4)
        copy(
            col_sum.at[:, pl.ds(0, WIDTH)], land_sum.at[z], 4, pos, lax.rem(there, 2) * 2 + core, there // 2
        ).start()
    copy(col_sum.at[:, pl.ds(WIDTH, 128)], land_den, 7, pos, cross, half).start()
    land_sum[z] = col_sum[:, :WIDTH]
    drains.append(lambda: done(land_sum.at[pl.ds(0, 3)], ssem.at[4]))
    drains.append(lambda: done(land_den, ssem.at[7]))

    @pl.when(giver)
    def _():
        done(land_x.at[pl.ds(0, BLK - 1)], rsem.at[2])

    @pl.when(jnp.logical_not(giver))
    def _():
        done(land_x, rsem.at[2])

    raw = [land_x[:, h].reshape(REP, WIDTH).astype(F32) for h in range(HALVES)]
    norm = jnp.sum(raw[0] * raw[0] + raw[1] * raw[1], axis=1, keepdims=True)
    inv = lax.rsqrt(norm + 1e-06)
    report = jnp.concatenate([(x * inv).astype(BF) for x in raw], axis=1)

    done(land_den, rsem.at[7])
    done(land_sum.at[pl.ds(0, 3)], rsem.at[4])
    both = [
        land_sum[2 * h].astype(F32) + land_sum[2 * h + 1].astype(F32) for h in range(HALVES)
    ]
    weights = col_sum[:, WIDTH:].astype(F32) + land_den[...].astype(F32)
    mean = [x / weights[:, :1] for x in both]
    norm = jnp.sum(mean[0] * mean[0] + mean[1] * mean[1], axis=1, keepdims=True)
    inv = lax.rsqrt(norm + 1e-06)
    unit = jnp.concatenate([(x * inv).astype(BF) for x in mean], axis=1)

    logits = scale[0] * nt(report, unit) + bias[0]
    i = lax.broadcasted_iota(jnp.int32, (REP, COL), 1)
    j = lax.broadcasted_iota(jnp.int32, (REP, COL), 0)
    study_id = pos * COL + i
    report_id = ((2 * (j // OWN) + lax.rem(half + core, 2)) * LANES + cross) * OWN + lax.rem(j, OWN)
    own = (study_id == report_id).astype(F32)
    slope = (jax.nn.sigmoid(logits) - own).astype(BF)

    odd = lax.rem(px + half + core, 2)
    for h in range(HALVES):
        text_part[h] = jnp.dot(slope, unit[:, h * WIDTH : (h + 1) * WIDTH], preferred_element_type=F32).astype(BF)
        for dy in (2, 1, 3, 0):
            for dx in (2, 0):
                p = at(dy, dx + odd)
                rows = pl.ds(pl.multiple_of((p // 2) * OWN, OWN), OWN)
                copy(text_part.at[h, rows], land_t.at[pos], 5, p, cross, h).start()
    drains.append(lambda: done(land_t, ssem.at[5]))

    gp = tn(slope, report).astype(BF)
    for h in range(HALVES):
        pooled_part[h] = gp[:, h * WIDTH : (h + 1) * WIDTH]
    me = lane * 2 + half
    for k in range(1, 8):
        there = lax.rem(me + k, 8)
        l, h = there // 2, lax.rem(there, 2)
        rows = pl.ds(pl.multiple_of(l * OWN, OWN), OWN)
        copy(pooled_part.at[h, rows], land_p.at[me], 6, pos, l, h).start()
    land_p[me] = pooled_part[half, pl.ds(pl.multiple_of(lane * OWN, OWN), OWN)]
    drains.append(lambda: done(land_p.at[pl.ds(0, 7)], ssem.at[6]))

    done(land_p.at[pl.ds(0, 7)], rsem.at[6])
    out_pooled[1] = jnp.zeros((OWN, WIDTH), BF)
    out_text[1] = jnp.zeros((OWN, WIDTH), BF)
    out_pooled[0] = jnp.sum(land_p[...].astype(F32), axis=0).astype(BF)
    done(land_t, rsem.at[5])
    out_text[0] = jnp.sum(land_t[...].astype(F32), axis=0).astype(BF)
    for drain in drains:
        drain()


def on_device(views, view_study, pool_query, texts, logit_scale, logit_bias):
    slots = views.shape[0]
    vmem = pl.BlockSpec(memory_space=pltpu.VMEM)
    hbm = pl.BlockSpec(memory_space=pltpu.HBM)
    smem = pl.BlockSpec(memory_space=pltpu.SMEM)
    out = jax.ShapeDtypeStruct((2, OWN, WIDTH), BF)
    res = pl.pallas_call(
        kernel,
        out_shape=(out, out),
        in_specs=[hbm, hbm, hbm, hbm, smem, smem],
        out_specs=(vmem, vmem),
        scratch_shapes=[
            pltpu.VMEM((slots, WIDTH), BF),
            pltpu.VMEM((1, slots), jnp.int32),
            pltpu.VMEM((WIDTH,), BF),
            pltpu.VMEM((OWN, WIDTH), BF),
            pltpu.VMEM((POS * CHUNK, PIECE), BF),
            pltpu.VMEM((POS * CHUNK, PIECE), BF),
            pltpu.VMEM((POS, 2, 128), F32),
            pltpu.VMEM((POS, 2, 128), F32),
            pltpu.VMEM((HALVES, OWN, WIDTH), BF),
            pltpu.VMEM((BLK, HALVES, OWN, WIDTH), BF),
            pltpu.VMEM((COL, WIDE), BF),
            pltpu.VMEM((COL, WIDE), BF),
            pltpu.VMEM((COL, WIDE), BF),
            pltpu.VMEM((4, COL, WIDTH), BF),
            pltpu.VMEM((COL, 128), BF),
            pltpu.VMEM((HALVES, REP, WIDTH), BF),
            pltpu.VMEM((HALVES, COL, WIDTH), BF),
            pltpu.VMEM((POS, OWN, WIDTH), BF),
            pltpu.VMEM((LANES * HALVES, OWN, WIDTH), BF),
            pltpu.SemaphoreType.DMA((9,)),
            pltpu.SemaphoreType.DMA((9,)),
            pltpu.SemaphoreType.DMA((4,)),
        ],
        compiler_params=pltpu.CompilerParams(
            collective_id=0, has_side_effects=True, vmem_limit_bytes=32 << 20
        ),
    )(
        *(pltpu.with_memory_space_constraint(x, pltpu.HBM) for x in (views, view_study.reshape(1, slots), pool_query, texts)),
        logit_scale, logit_bias,
    )
    zero = jnp.zeros((), BF)
    return tuple(
        lax.reduce(tuple(res), (zero, zero), lambda a, b: (a[0] + b[0], a[1] + b[1]), (0,))
    )


def solution(mesh):
    in_specs = (P("dp", "mp"), P("dp"), P("mp"), P("dp", "mp"), P(), P())
    out_specs = (P("dp", "mp"), P("dp", "mp"))
    return jax.shard_map(
        on_device, mesh=mesh, in_specs=in_specs, out_specs=out_specs, check_vma=False
    )
```

```python
import jax
import jax.numpy as jnp
from jax import lax
from jax.experimental import pallas as pl
from jax.experimental.pallas import tpu as pltpu
from jax.sharding import PartitionSpec as P

MESH = pl.DeviceIdType.MESH
BF, F32 = jnp.bfloat16, jnp.float32
SIDE = 4
POS, LANES, HALVES, CORES = 16, 4, 2, 2
OWN = 16
WIDTH = 512
SLOTS = 8
COL = LANES * OWN
BLK = 8
REP = BLK * OWN
PIECE = WIDTH // 2
CHUNK = 2 * SLOTS
WIDE = WIDTH + 128

NEAR = {0: 0, 1: 1, 2: 2, 3: 1}
STEPS = sorted(
    ((dy, dx) for dy in range(SIDE) for dx in range(SIDE)), key=lambda s: -NEAR[s[0]] - NEAR[s[1]]
)


def nt(a, b):
    return lax.dot_general(a, b, (((1,), (1,)), ((), ())), preferred_element_type=F32)


def tn(a, b):
    return lax.dot_general(a, b, (((0,), (0,)), ((), ())), preferred_element_type=F32)


def kernel(
    views_in, study_in, query_in, texts_in, scale, bias, out_pooled, out_text,
    views, study, query, texts, send_v, land_v, send_s, land_s, land_r, land_x, part, land_sib, col_sum, land_sum,
    land_den, text_part, pooled_part, pooled_sum, land_q, land_t, land_p, ssem, rsem, lsem,
):
    dp, half = lax.axis_index("dp"), lax.axis_index("mp")
    pos, lane = lax.div(dp, LANES), lax.rem(dp, LANES)
    py, px = lax.div(pos, SIDE), lax.rem(pos, SIDE)
    zlo, core = lax.div(lane, 2), lax.rem(lane, 2)
    other = 1 - half
    cross = (1 - zlo) * 2 + core

    rows_of = [lax.rem(py + d, SIDE) * SIDE for d in range(SIDE)]
    columns_of = [lax.rem(px + d, SIDE) for d in range(SIDE)]

    def at(dy, dx):
        return rows_of[dy] + columns_of[dx]

    loads = [
        pltpu.make_async_copy(a, b, lsem.at[i])
        for i, (a, b) in enumerate(
            [(study_in, study), (views_in, views), (query_in, query), (texts_in, texts)]
        )
    ]
    for load in loads:
        load.start()
    barrier = pltpu.get_barrier_semaphore()

    def greet(p, l, h):
        pl.semaphore_signal(barrier, inc=1, device_id=(p * LANES + l, h), device_id_type=MESH)

    for dy, dx in STEPS:
        greet(at(dy, dx), lane, other)
    for dy, dx in STEPS[:-1]:
        greet(at(dy, dx), lane, half)
    for k in range(1, LANES):
        for h in (other, half):
            greet(pos, lax.rem(lane + k, LANES), h)

    drains = []

    loads[0].wait()
    slots = views.shape[0]
    row = lax.broadcasted_iota(jnp.int32, (slots, slots), 0)
    colm = lax.broadcasted_iota(jnp.int32, (slots, slots), 1)
    ids = study[...]
    mine = (ids >> 4) == (row >> 1)
    before = (row < colm).astype(F32).astype(BF)
    hot = mine.astype(F32).astype(BF)
    rank = jnp.dot(hot, before, preferred_element_type=F32)
    chosen = mine & (rank == (row & 1).astype(F32))
    pick = chosen.astype(F32).astype(BF)
    loads[1].wait()
    packed = jnp.dot(pick, views[...], preferred_element_type=F32)
    loads[2].wait()
    asked = query[...].reshape(1, WIDTH).astype(F32)
    score = nt(jnp.broadcast_to(asked, (SLOTS, WIDTH)).astype(BF), views[...])[:1]
    mark = ((ids & (COL - 1)) + 1).astype(F32)
    wide_row = lax.broadcasted_iota(jnp.int32, (slots, POS * CHUNK), 0)
    wide_col = lax.broadcasted_iota(jnp.int32, (slots, POS * CHUNK), 1)
    place = (colm // CHUNK == lax.rem(pos, 8)) & ((colm & (SLOTS - 1)) == (row & (SLOTS - 1)))
    for k, x in enumerate((score, mark)):
        x = jnp.sum(jnp.where(chosen, x, 0.0), axis=1, keepdims=True)
        send_s[:, k, :] = jnp.sum(jnp.where(place, x, 0.0).reshape(POS, SLOTS, 128), axis=1)
    parts = [packed[:, q * PIECE : (q + 1) * PIECE] for q in range(2)]
    ask = jnp.concatenate(
        [jnp.broadcast_to(asked[:, q * PIECE : (q + 1) * PIECE], (SLOTS, PIECE)) for q in range(2)], axis=0
    ).astype(BF)
    chunks = jnp.concatenate([x.reshape(POS, 1, SLOTS, PIECE) for x in parts], axis=1)
    send_v[...] = chunks.reshape(POS * CHUNK, PIECE).astype(BF)
    mine_rows = pl.ds(pl.multiple_of(pos * CHUNK, CHUNK), CHUNK)
    land_v[mine_rows] = send_v[mine_rows]
    pl.semaphore_wait(barrier, 2 * POS - 1 + 6)

    def copy(src, dst, i, p, l, h):
        return pltpu.make_async_remote_copy(
            src_ref=src, dst_ref=dst, send_sem=ssem.at[i], recv_sem=rsem.at[i],
            device_id=(p * LANES + l, h), device_id_type=MESH,
        )

    def done(ref, sem):
        pltpu.make_async_copy(ref, ref, sem).wait()

    sel = lax.rem(pos + core, 2)
    giver = sel == half
    loads[3].wait()
    copy(texts, land_r.at[half], 8, pos, cross, sel).start()
    drains.append(lambda: done(texts, ssem.at[8]))
    for dy, dx in STEPS:
        p = at(dy, dx)
        copy(send_s.at[p], land_s.at[pos], 1, p, lane, other).start()
    for dy, dx in STEPS[:-1]:
        p = at(dy, dx)
        copy(
            send_v.at[pl.ds(pl.multiple_of(p * CHUNK, CHUNK), CHUNK)],
            land_v.at[mine_rows], 0, p, lane, half,
        ).start()
    drains.append(lambda: done(send_v.at[pl.ds(0, (POS - 1) * CHUNK)], ssem.at[0]))
    drains.append(lambda: done(send_s, ssem.at[1]))

    done(land_v.at[pl.ds(0, (POS - 1) * CHUNK)], rsem.at[0])
    held = land_v[...]
    second = (lax.broadcasted_iota(jnp.int32, (1, POS * CHUNK), 1) & SLOTS) != 0
    piece = nt(ask, held)
    piece = jnp.where(second, piece[SLOTS : SLOTS + 1], piece[:1])
    rest = jnp.where(second, pltpu.roll(piece, SLOTS, 1), pltpu.roll(piece, POS * CHUNK - SLOTS, 1))

    @pl.when(giver)
    def _():
        done(land_r, rsem.at[8])
        for dy, dx in STEPS[:-1]:
            copy(land_r, land_x.at[pos // 2], 2, at(dy, dx), lane, half).start()
        land_x[pos // 2] = land_r[...]

    def handed():
        @pl.when(giver)
        def _():
            done(land_x, ssem.at[2])
            done(land_x.at[pl.ds(0, BLK - 1)], ssem.at[2])

    drains.append(handed)

    done(land_s, rsem.at[1])
    more = jnp.sum(land_s[...].reshape(2, 8, 2, 128), axis=1)
    more = jnp.concatenate([more[0], more[1]], axis=1)
    weight = jax.nn.sigmoid(piece + rest + more[:1]).astype(BF).astype(F32)
    study_row = (wide_row & (COL - 1)) + 1
    fits = (more[1:] == study_row.astype(F32)) & (((wide_row & COL) != 0) == ((wide_col & SLOTS) != 0))
    table = jnp.where(fits, weight, 0.0).astype(BF)
    sums = jnp.dot(table, held, preferred_element_type=F32)
    total = jnp.dot(table[:COL], jnp.ones((POS * CHUNK, 128), BF), preferred_element_type=F32)
    sums = jnp.concatenate([sums[:COL], sums[COL:], total], axis=1)
    part[...] = sums.astype(BF)
    sib = copy(part, land_sib, 3, pos, lane + 1 - 2 * core, half)
    sib.start()
    sib.wait_recv()
    drains.append(sib.wait_send)
    col_sum[...] = (sums + land_sib[...].astype(F32)).astype(BF)
    z = half * 2 + zlo
    for k in (2, 1, 3):
        there = lax.rem(z + k, 4)
        copy(
            col_sum.at[:, pl.ds(0, WIDTH)], land_sum.at[z], 4, pos, lax.rem(there, 2) * 2 + core, there // 2
        ).start()
    copy(col_sum.at[:, pl.ds(WIDTH, 128)], land_den, 7, pos, cross, half).start()
    land_sum[z] = col_sum[:, :WIDTH]
    drains.append(lambda: done(land_sum.at[pl.ds(0, 3)], ssem.at[4]))
    drains.append(lambda: done(land_den, ssem.at[7]))

    @pl.when(giver)
    def _():
        done(land_x.at[pl.ds(0, BLK - 1)], rsem.at[2])

    @pl.when(jnp.logical_not(giver))
    def _():
        done(land_x, rsem.at[2])

    raw = [land_x[:, h].reshape(REP, WIDTH).astype(F32) for h in range(HALVES)]
    norm = jnp.sum(raw[0] * raw[0] + raw[1] * raw[1], axis=1, keepdims=True)
    inv = lax.rsqrt(norm + 1e-06)
    report = jnp.concatenate([(x * inv).astype(BF) for x in raw], axis=1)

    done(land_den, rsem.at[7])
    done(land_sum.at[pl.ds(0, 3)], rsem.at[4])
    both = [
        land_sum[2 * h].astype(F32) + land_sum[2 * h + 1].astype(F32) for h in range(HALVES)
    ]
    weights = col_sum[:, WIDTH:].astype(F32) + land_den[...].astype(F32)
    share = 1.0 / weights[:, :1]
    mean = [x * share for x in both]
    norm = jnp.sum(mean[0] * mean[0] + mean[1] * mean[1], axis=1, keepdims=True)
    inv = lax.rsqrt(norm + 1e-06)
    unit = jnp.concatenate([(x * inv).astype(BF) for x in mean], axis=1)

    logits = scale[0] * nt(report, unit) + bias[0]
    i = lax.broadcasted_iota(jnp.int32, (REP, COL), 1)
    j = lax.broadcasted_iota(jnp.int32, (REP, COL), 0)
    study_id = pos * COL + i
    report_id = ((2 * (j // OWN) + lax.rem(half + core, 2)) * LANES + cross) * OWN + lax.rem(j, OWN)
    own = (study_id == report_id).astype(F32)
    slope = (jax.nn.sigmoid(logits) - own).astype(BF)

    odd = lax.rem(px + half + core, 2)
    odd_column = lax.rem(half + core, 2)
    given = [(y, lax.rem(px + dx + odd, SIDE)) for y in (rows_of[2], rows_of[1], rows_of[3], rows_of[0]) for dx in (2, 0)]
    for h in range(HALVES):
        text_part[h] = jnp.dot(slope, unit[:, h * WIDTH : (h + 1) * WIDTH], preferred_element_type=F32).astype(BF)
        for y, x in given:
            rows = pl.ds(pl.multiple_of((y + x - odd_column) * BLK, OWN), OWN)
            copy(text_part.at[h, rows], land_t.at[pos], 5, y + x, cross, h).start()
    drains.append(lambda: done(land_t, ssem.at[5]))

    gp = tn(slope, report).astype(BF)
    for h in range(HALVES):
        pooled_part[h] = gp[:, h * WIDTH : (h + 1) * WIDTH].reshape(2, CORES, OWN, WIDTH)
    pair = copy(pooled_part.at[:, :, 1 - core], land_q, 9, pos, lane + 1 - 2 * core, half)
    pair.start()
    drains.append(pair.wait_send)
    pair.wait_recv()
    pooled_sum[...] = (pooled_part[:, :, core].astype(F32) + land_q[...].astype(F32)).astype(BF)
    for k in (2, 1, 3):
        there = lax.rem(z + k, 4)
        h, l = lax.div(there, 2), lax.rem(there, 2)
        copy(pooled_sum.at[h, l], land_p.at[z], 6, pos, l * 2 + core, h).start()
    land_p[z] = pooled_sum[half, zlo]
    drains.append(lambda: done(land_p.at[pl.ds(0, 3)], ssem.at[6]))

    done(land_p.at[pl.ds(0, 3)], rsem.at[6])
    out_pooled[1] = jnp.zeros((OWN, WIDTH), BF)
    out_text[1] = jnp.zeros((OWN, WIDTH), BF)
    out_pooled[0] = jnp.sum(land_p[...].astype(F32), axis=0).astype(BF)
    done(land_t, rsem.at[5])
    out_text[0] = jnp.sum(land_t[...].astype(F32), axis=0).astype(BF)
    for drain in drains:
        drain()


def on_device(views, view_study, pool_query, texts, logit_scale, logit_bias):
    slots = views.shape[0]
    vmem = pl.BlockSpec(memory_space=pltpu.VMEM)
    hbm = pl.BlockSpec(memory_space=pltpu.HBM)
    smem = pl.BlockSpec(memory_space=pltpu.SMEM)
    out = jax.ShapeDtypeStruct((2, OWN, WIDTH), BF)
    res = pl.pallas_call(
        kernel,
        out_shape=(out, out),
        in_specs=[hbm, hbm, hbm, hbm, smem, smem],
        out_specs=(vmem, vmem),
        scratch_shapes=[
            pltpu.VMEM((slots, WIDTH), BF),
            pltpu.VMEM((1, slots), jnp.int32),
            pltpu.VMEM((WIDTH,), BF),
            pltpu.VMEM((OWN, WIDTH), BF),
            pltpu.VMEM((POS * CHUNK, PIECE), BF),
            pltpu.VMEM((POS * CHUNK, PIECE), BF),
            pltpu.VMEM((POS, 2, 128), F32),
            pltpu.VMEM((POS, 2, 128), F32),
            pltpu.VMEM((HALVES, OWN, WIDTH), BF),
            pltpu.VMEM((BLK, HALVES, OWN, WIDTH), BF),
            pltpu.VMEM((COL, WIDE), BF),
            pltpu.VMEM((COL, WIDE), BF),
            pltpu.VMEM((COL, WIDE), BF),
            pltpu.VMEM((4, COL, WIDTH), BF),
            pltpu.VMEM((COL, 128), BF),
            pltpu.VMEM((HALVES, REP, WIDTH), BF),
            pltpu.VMEM((HALVES, 2, CORES, OWN, WIDTH), BF),
            pltpu.VMEM((HALVES, 2, OWN, WIDTH), BF),
            pltpu.VMEM((HALVES, 2, OWN, WIDTH), BF),
            pltpu.VMEM((POS, OWN, WIDTH), BF),
            pltpu.VMEM((4, OWN, WIDTH), BF),
            pltpu.SemaphoreType.DMA((10,)),
            pltpu.SemaphoreType.DMA((10,)),
            pltpu.SemaphoreType.DMA((4,)),
        ],
        compiler_params=pltpu.CompilerParams(
            collective_id=0, has_side_effects=True, vmem_limit_bytes=32 << 20
        ),
    )(
        *(pltpu.with_memory_space_constraint(x, pltpu.HBM) for x in (views, view_study.reshape(1, slots), pool_query, texts)),
        logit_scale, logit_bias,
    )
    zero = jnp.zeros((), BF)
    return tuple(
        lax.reduce(tuple(res), (zero, zero), lambda a, b: (a[0] + b[0], a[1] + b[1]), (0,))
    )


def solution(mesh):
    in_specs = (P("dp", "mp"), P("dp"), P("mp"), P("dp", "mp"), P(), P())
    out_specs = (P("dp", "mp"), P("dp", "mp"))
    return jax.shard_map(
        on_device, mesh=mesh, in_specs=in_specs, out_specs=out_specs, check_vma=False
    )
```

```python
import jax
import jax.numpy as jnp
from jax import lax
from jax.experimental import pallas as pl
from jax.experimental.pallas import tpu as pltpu
from jax.sharding import PartitionSpec as P

MESH = pl.DeviceIdType.MESH
BF, F32 = jnp.bfloat16, jnp.float32
SIDE = 4
POS, LANES, HALVES, CORES = 16, 4, 2, 2
OWN = 16
WIDTH = 512
SLOTS = 8
COL = LANES * OWN
BLK = 8
REP = BLK * OWN
PIECE = WIDTH // 2
CHUNK = 2 * SLOTS
WIDE = WIDTH + 128

NEAR = {0: 0, 1: 1, 2: 2, 3: 1}
STEPS = sorted(
    ((dy, dx) for dy in range(SIDE) for dx in range(SIDE)), key=lambda s: -NEAR[s[0]] - NEAR[s[1]]
)


def nt(a, b):
    return lax.dot_general(a, b, (((1,), (1,)), ((), ())), preferred_element_type=F32)


def tn(a, b):
    return lax.dot_general(a, b, (((0,), (0,)), ((), ())), preferred_element_type=F32)


def kernel(
    views_in, study_in, query_in, texts_in, scale, bias, out_pooled, out_text,
    views, study, query, texts, send_v, land_v, send_s, land_s, land_r, land_x, part, land_sib, col_sum, land_sum,
    land_den, text_part, pooled_part, pooled_sum, land_q, land_t, land_p, ssem, rsem, lsem,
):
    dp, half = lax.axis_index("dp"), lax.axis_index("mp")
    pos, lane = lax.div(dp, LANES), lax.rem(dp, LANES)
    py, px = lax.div(pos, SIDE), lax.rem(pos, SIDE)
    zlo, core = lax.div(lane, 2), lax.rem(lane, 2)
    other = 1 - half
    cross = (1 - zlo) * 2 + core

    rows_of = [lax.rem(py + d, SIDE) * SIDE for d in range(SIDE)]
    columns_of = [lax.rem(px + d, SIDE) for d in range(SIDE)]

    def at(dy, dx):
        return rows_of[dy] + columns_of[dx]

    loads = [
        pltpu.make_async_copy(a, b, lsem.at[i])
        for i, (a, b) in enumerate(
            [(study_in, study), (views_in, views), (query_in, query), (texts_in, texts)]
        )
    ]
    for load in loads:
        load.start()
    barrier = pltpu.get_barrier_semaphore()

    def greet(p, l, h):
        pl.semaphore_signal(barrier, inc=1, device_id=(p * LANES + l, h), device_id_type=MESH)

    for dy, dx in STEPS:
        greet(at(dy, dx), lane, other)
    for dy, dx in STEPS[:-1]:
        greet(at(dy, dx), lane, half)
    for k in range(1, LANES):
        for h in (other, half):
            greet(pos, lax.rem(lane + k, LANES), h)

    drains = []

    loads[0].wait()
    slots = views.shape[0]
    row = lax.broadcasted_iota(jnp.int32, (slots, slots), 0)
    colm = lax.broadcasted_iota(jnp.int32, (slots, slots), 1)
    ids = study[...]
    mine = (ids >> 4) == (row >> 1)
    before = (row < colm).astype(F32).astype(BF)
    hot = mine.astype(F32).astype(BF)
    rank = jnp.dot(hot, before, preferred_element_type=F32)
    chosen = mine & (rank == (row & 1).astype(F32))
    pick = chosen.astype(F32).astype(BF)
    loads[1].wait()
    packed = jnp.dot(pick, views[...], preferred_element_type=F32)
    loads[2].wait()
    asked = query[...].reshape(1, WIDTH).astype(F32)
    score = nt(jnp.broadcast_to(asked, (SLOTS, WIDTH)).astype(BF), views[...])[:1]
    mark = ((ids & (COL - 1)) + 1).astype(F32)
    wide_row = lax.broadcasted_iota(jnp.int32, (slots, POS * CHUNK), 0)
    wide_col = lax.broadcasted_iota(jnp.int32, (slots, POS * CHUNK), 1)
    place = (colm // CHUNK == lax.rem(pos, 8)) & ((colm & (SLOTS - 1)) == (row & (SLOTS - 1)))
    for k, x in enumerate((score, mark)):
        x = jnp.sum(jnp.where(chosen, x, 0.0), axis=1, keepdims=True)
        send_s[:, k, :] = jnp.sum(jnp.where(place, x, 0.0).reshape(POS, SLOTS, 128), axis=1)
    parts = [packed[:, q * PIECE : (q + 1) * PIECE] for q in range(2)]
    ask = jnp.concatenate(
        [jnp.broadcast_to(asked[:, q * PIECE : (q + 1) * PIECE], (SLOTS, PIECE)) for q in range(2)], axis=0
    ).astype(BF)
    chunks = jnp.concatenate([x.reshape(POS, 1, SLOTS, PIECE) for x in parts], axis=1)
    send_v[...] = chunks.reshape(POS * CHUNK, PIECE).astype(BF)
    mine_rows = pl.ds(pl.multiple_of(pos * CHUNK, CHUNK), CHUNK)
    land_v[mine_rows] = send_v[mine_rows]
    pl.semaphore_wait(barrier, 2 * POS - 1 + 6)

    def copy(src, dst, i, p, l, h):
        return pltpu.make_async_remote_copy(
            src_ref=src, dst_ref=dst, send_sem=ssem.at[i], recv_sem=rsem.at[i],
            device_id=(p * LANES + l, h), device_id_type=MESH,
        )

    def done(ref, sem):
        pltpu.make_async_copy(ref, ref, sem).wait()

    sel = lax.rem(pos + core, 2)
    giver = sel == half
    loads[3].wait()
    copy(texts, land_r.at[half], 8, pos, cross, sel).start()
    drains.append(lambda: done(texts, ssem.at[8]))
    for dy, dx in STEPS:
        p = at(dy, dx)
        copy(send_s.at[p], land_s.at[pos], 1, p, lane, other).start()
    for dy, dx in STEPS[:-1]:
        p = at(dy, dx)
        copy(
            send_v.at[pl.ds(pl.multiple_of(p * CHUNK, CHUNK), CHUNK)],
            land_v.at[mine_rows], 0, p, lane, half,
        ).start()
    drains.append(lambda: done(send_v.at[pl.ds(0, (POS - 1) * CHUNK)], ssem.at[0]))
    drains.append(lambda: done(send_s, ssem.at[1]))

    @pl.when(giver)
    def _():
        done(land_r, rsem.at[8])
        for dy, dx in STEPS[:8]:
            copy(land_r, land_x.at[pos // 2], 2, at(dy, dx), lane, half).start()
        land_x[pos // 2] = land_r[...]

    def handed():
        @pl.when(giver)
        def _():
            done(land_x, ssem.at[2])
            done(land_x.at[pl.ds(0, BLK - 1)], ssem.at[2])

    drains.append(handed)

    done(land_v.at[pl.ds(0, (POS - 1) * CHUNK)], rsem.at[0])
    held = land_v[...]
    second = (lax.broadcasted_iota(jnp.int32, (1, POS * CHUNK), 1) & SLOTS) != 0
    piece = nt(ask, held)
    piece = jnp.where(second, piece[SLOTS : SLOTS + 1], piece[:1])
    rest = jnp.where(second, pltpu.roll(piece, SLOTS, 1), pltpu.roll(piece, POS * CHUNK - SLOTS, 1))

    @pl.when(giver)
    def _():
        for dy, dx in STEPS[8:-1]:
            copy(land_r, land_x.at[pos // 2], 2, at(dy, dx), lane, half).start()

    done(land_s, rsem.at[1])
    more = jnp.sum(land_s[...].reshape(2, 8, 2, 128), axis=1)
    more = jnp.concatenate([more[0], more[1]], axis=1)
    weight = jax.nn.sigmoid(piece + rest + more[:1]).astype(BF).astype(F32)
    study_row = (wide_row & (COL - 1)) + 1
    fits = (more[1:] == study_row.astype(F32)) & (((wide_row & COL) != 0) == ((wide_col & SLOTS) != 0))
    table = jnp.where(fits, weight, 0.0).astype(BF)
    sums = jnp.dot(table, held, preferred_element_type=F32)
    total = jnp.dot(table[:COL], jnp.ones((POS * CHUNK, 128), BF), preferred_element_type=F32)
    sums = jnp.concatenate([sums[:COL], sums[COL:], total], axis=1)
    part[...] = sums.astype(BF)
    sib = copy(part, land_sib, 3, pos, lane + 1 - 2 * core, half)
    sib.start()
    sib.wait_recv()
    drains.append(sib.wait_send)
    col_sum[...] = (sums + land_sib[...].astype(F32)).astype(BF)
    z = half * 2 + zlo
    for k in (2, 1, 3):
        there = lax.rem(z + k, 4)
        copy(
            col_sum.at[:, pl.ds(0, WIDTH)], land_sum.at[z], 4, pos, lax.rem(there, 2) * 2 + core, there // 2
        ).start()
    copy(col_sum.at[:, pl.ds(WIDTH, 128)], land_den, 7, pos, cross, half).start()
    land_sum[z] = col_sum[:, :WIDTH]
    drains.append(lambda: done(land_sum.at[pl.ds(0, 3)], ssem.at[4]))
    drains.append(lambda: done(land_den, ssem.at[7]))

    @pl.when(giver)
    def _():
        done(land_x.at[pl.ds(0, BLK - 1)], rsem.at[2])

    @pl.when(jnp.logical_not(giver))
    def _():
        done(land_x, rsem.at[2])

    raw = [land_x[:, h].reshape(REP, WIDTH).astype(F32) for h in range(HALVES)]
    norm = jnp.sum(raw[0] * raw[0] + raw[1] * raw[1], axis=1, keepdims=True)
    inv = lax.rsqrt(norm + 1e-06)
    report = jnp.concatenate([(x * inv).astype(BF) for x in raw], axis=1)

    done(land_den, rsem.at[7])
    done(land_sum.at[pl.ds(0, 3)], rsem.at[4])
    both = [
        land_sum[2 * h].astype(F32) + land_sum[2 * h + 1].astype(F32) for h in range(HALVES)
    ]
    weights = col_sum[:, WIDTH:].astype(F32) + land_den[...].astype(F32)
    share = 1.0 / weights[:, :1]
    mean = [x * share for x in both]
    norm = jnp.sum(mean[0] * mean[0] + mean[1] * mean[1], axis=1, keepdims=True)
    inv = lax.rsqrt(norm + 1e-06)
    unit = jnp.concatenate([(x * inv).astype(BF) for x in mean], axis=1)

    logits = scale[0] * nt(report, unit) + bias[0]
    i = lax.broadcasted_iota(jnp.int32, (REP, COL), 1)
    j = lax.broadcasted_iota(jnp.int32, (REP, COL), 0)
    study_id = pos * COL + i
    report_id = ((2 * (j // OWN) + lax.rem(half + core, 2)) * LANES + cross) * OWN + lax.rem(j, OWN)
    own = (study_id == report_id).astype(F32)
    slope = (jax.nn.sigmoid(logits) - own).astype(BF)

    odd = lax.rem(px + half + core, 2)
    odd_column = lax.rem(half + core, 2)
    given = [(y, lax.rem(px + dx + odd, SIDE)) for y in (rows_of[2], rows_of[1], rows_of[3], rows_of[0]) for dx in (2, 0)]
    for h in (0,):
        text_part[h] = jnp.dot(slope, unit[:, h * WIDTH : (h + 1) * WIDTH], preferred_element_type=F32).astype(BF)
        for y, x in given:
            rows = pl.ds(pl.multiple_of((y + x - odd_column) * BLK, OWN), OWN)
            copy(text_part.at[h, rows], land_t.at[pos], 5, y + x, cross, h).start()
    drains.append(lambda: done(land_t, ssem.at[5]))

    gp = tn(slope, report).astype(BF)
    for h in range(HALVES):
        pooled_part[h] = gp[:, h * WIDTH : (h + 1) * WIDTH].reshape(2, CORES, OWN, WIDTH)
    pair = copy(pooled_part.at[:, :, 1 - core], land_q, 9, pos, lane + 1 - 2 * core, half)
    pair.start()
    for h in (1,):
        text_part[h] = jnp.dot(slope, unit[:, h * WIDTH : (h + 1) * WIDTH], preferred_element_type=F32).astype(BF)
        for y, x in given:
            rows = pl.ds(pl.multiple_of((y + x - odd_column) * BLK, OWN), OWN)
            copy(text_part.at[h, rows], land_t.at[pos], 5, y + x, cross, h).start()
    drains.append(pair.wait_send)
    pair.wait_recv()
    pooled_sum[...] = (pooled_part[:, :, core].astype(F32) + land_q[...].astype(F32)).astype(BF)
    for k in (2, 1, 3):
        there = lax.rem(z + k, 4)
        h, l = lax.div(there, 2), lax.rem(there, 2)
        copy(pooled_sum.at[h, l], land_p.at[z], 6, pos, l * 2 + core, h).start()
    land_p[z] = pooled_sum[half, zlo]
    drains.append(lambda: done(land_p.at[pl.ds(0, 3)], ssem.at[6]))

    done(land_p.at[pl.ds(0, 3)], rsem.at[6])
    out_pooled[1] = jnp.zeros((OWN, WIDTH), BF)
    out_text[1] = jnp.zeros((OWN, WIDTH), BF)
    out_pooled[0] = jnp.sum(land_p[...].astype(F32), axis=0).astype(BF)
    done(land_t, rsem.at[5])
    out_text[0] = jnp.sum(land_t[...].astype(F32), axis=0).astype(BF)
    for drain in drains:
        drain()


def on_device(views, view_study, pool_query, texts, logit_scale, logit_bias):
    slots = views.shape[0]
    vmem = pl.BlockSpec(memory_space=pltpu.VMEM)
    hbm = pl.BlockSpec(memory_space=pltpu.HBM)
    smem = pl.BlockSpec(memory_space=pltpu.SMEM)
    out = jax.ShapeDtypeStruct((2, OWN, WIDTH), BF)
    res = pl.pallas_call(
        kernel,
        out_shape=(out, out),
        in_specs=[hbm, hbm, hbm, hbm, smem, smem],
        out_specs=(vmem, vmem),
        scratch_shapes=[
            pltpu.VMEM((slots, WIDTH), BF),
            pltpu.VMEM((1, slots), jnp.int32),
            pltpu.VMEM((WIDTH,), BF),
            pltpu.VMEM((OWN, WIDTH), BF),
            pltpu.VMEM((POS * CHUNK, PIECE), BF),
            pltpu.VMEM((POS * CHUNK, PIECE), BF),
            pltpu.VMEM((POS, 2, 128), F32),
            pltpu.VMEM((POS, 2, 128), F32),
            pltpu.VMEM((HALVES, OWN, WIDTH), BF),
            pltpu.VMEM((BLK, HALVES, OWN, WIDTH), BF),
            pltpu.VMEM((COL, WIDE), BF),
            pltpu.VMEM((COL, WIDE), BF),
            pltpu.VMEM((COL, WIDE), BF),
            pltpu.VMEM((4, COL, WIDTH), BF),
            pltpu.VMEM((COL, 128), BF),
            pltpu.VMEM((HALVES, REP, WIDTH), BF),
            pltpu.VMEM((HALVES, 2, CORES, OWN, WIDTH), BF),
            pltpu.VMEM((HALVES, 2, OWN, WIDTH), BF),
            pltpu.VMEM((HALVES, 2, OWN, WIDTH), BF),
            pltpu.VMEM((POS, OWN, WIDTH), BF),
            pltpu.VMEM((4, OWN, WIDTH), BF),
            pltpu.SemaphoreType.DMA((10,)),
            pltpu.SemaphoreType.DMA((10,)),
            pltpu.SemaphoreType.DMA((4,)),
        ],
        compiler_params=pltpu.CompilerParams(
            collective_id=0, has_side_effects=True, vmem_limit_bytes=32 << 20
        ),
    )(
        *(pltpu.with_memory_space_constraint(x, pltpu.HBM) for x in (views, view_study.reshape(1, slots), pool_query, texts)),
        logit_scale, logit_bias,
    )
    zero = jnp.zeros((), BF)
    return tuple(
        lax.reduce(tuple(res), (zero, zero), lambda a, b: (a[0] + b[0], a[1] + b[1]), (0,))
    )


def solution(mesh):
    in_specs = (P("dp", "mp"), P("dp"), P("mp"), P("dp", "mp"), P(), P())
    out_specs = (P("dp", "mp"), P("dp", "mp"))
    return jax.shard_map(
        on_device, mesh=mesh, in_specs=in_specs, out_specs=out_specs, check_vma=False
    )
```

```python
import jax
import jax.numpy as jnp
from jax import lax
from jax.experimental import pallas as pl
from jax.experimental.pallas import tpu as pltpu
from jax.sharding import PartitionSpec as P

MESH = pl.DeviceIdType.MESH
BF, F32 = jnp.bfloat16, jnp.float32
SIDE = 4
POS, LANES, HALVES, CORES = 16, 4, 2, 2
OWN = 16
WIDTH = 512
SLOTS = 8
COL = LANES * OWN
BLK = 8
REP = BLK * OWN
PIECE = WIDTH // 2
CHUNK = 2 * SLOTS
WIDE = WIDTH + 128

NEAR = {0: 0, 1: 1, 2: 2, 3: 1}
STEPS = sorted(
    ((dy, dx) for dy in range(SIDE) for dx in range(SIDE)), key=lambda s: -NEAR[s[0]] - NEAR[s[1]]
)


def nt(a, b):
    return lax.dot_general(a, b, (((1,), (1,)), ((), ())), preferred_element_type=F32)


def tn(a, b):
    return lax.dot_general(a, b, (((0,), (0,)), ((), ())), preferred_element_type=F32)


def kernel(
    views_in, study_in, query_in, texts_in, scale, bias, out_pooled, out_text,
    views, study, query, texts, send_v, land_v, send_s, land_s, land_r, land_x, part, land_sib, col_sum, land_sum,
    land_den, text_part, pooled_part, pooled_sum, land_q, land_t, land_p, ssem, rsem, lsem,
):
    dp, half = lax.axis_index("dp"), lax.axis_index("mp")
    pos, lane = lax.div(dp, LANES), lax.rem(dp, LANES)
    py, px = lax.div(pos, SIDE), lax.rem(pos, SIDE)
    zlo, core = lax.div(lane, 2), lax.rem(lane, 2)
    other = 1 - half
    cross = (1 - zlo) * 2 + core

    rows_of = [lax.rem(py + d, SIDE) * SIDE for d in range(SIDE)]
    columns_of = [lax.rem(px + d, SIDE) for d in range(SIDE)]

    def at(dy, dx):
        return rows_of[dy] + columns_of[dx]

    loads = [
        pltpu.make_async_copy(a, b, lsem.at[i])
        for i, (a, b) in enumerate(
            [(study_in, study), (views_in, views), (query_in, query), (texts_in, texts)]
        )
    ]
    for load in loads:
        load.start()
    barrier = pltpu.get_barrier_semaphore()

    def greet(p, l, h):
        pl.semaphore_signal(barrier, inc=1, device_id=(p * LANES + l, h), device_id_type=MESH)

    for dy, dx in STEPS:
        greet(at(dy, dx), lane, other)
    for dy, dx in STEPS[:-1]:
        greet(at(dy, dx), lane, half)
    for k in range(1, LANES):
        for h in (other, half):
            greet(pos, lax.rem(lane + k, LANES), h)

    drains = []

    loads[0].wait()
    slots = views.shape[0]
    row = lax.broadcasted_iota(jnp.int32, (slots, slots), 0)
    colm = lax.broadcasted_iota(jnp.int32, (slots, slots), 1)
    ids = study[...]
    mine = (ids >> 4) == (row >> 1)
    before = (row < colm).astype(F32).astype(BF)
    hot = mine.astype(F32).astype(BF)
    rank = jnp.dot(hot, before, preferred_element_type=F32)
    chosen = mine & (rank == (row & 1).astype(F32))
    pick = chosen.astype(F32).astype(BF)
    loads[1].wait()
    packed = jnp.dot(pick, views[...], preferred_element_type=F32)
    loads[2].wait()
    asked = query[...].reshape(1, WIDTH).astype(F32)
    score = nt(jnp.broadcast_to(asked, (SLOTS, WIDTH)).astype(BF), views[...])[:1]
    mark = ((ids & (COL - 1)) + 1).astype(F32)
    wide_row = lax.broadcasted_iota(jnp.int32, (slots, POS * CHUNK), 0)
    wide_col = lax.broadcasted_iota(jnp.int32, (slots, POS * CHUNK), 1)
    place = (colm // CHUNK == lax.rem(pos, 8)) & ((colm & (SLOTS - 1)) == (row & (SLOTS - 1)))
    for k, x in enumerate((score, mark)):
        x = jnp.sum(jnp.where(chosen, x, 0.0), axis=1, keepdims=True)
        send_s[:, k, :] = jnp.sum(jnp.where(place, x, 0.0).reshape(POS, SLOTS, 128), axis=1)
    parts = [packed[:, q * PIECE : (q + 1) * PIECE] for q in range(2)]
    ask = jnp.concatenate(
        [jnp.broadcast_to(asked[:, q * PIECE : (q + 1) * PIECE], (SLOTS, PIECE)) for q in range(2)], axis=0
    ).astype(BF)
    chunks = jnp.concatenate([x.reshape(POS, 1, SLOTS, PIECE) for x in parts], axis=1)
    send_v[...] = chunks.reshape(POS * CHUNK, PIECE).astype(BF)
    mine_rows = pl.ds(pl.multiple_of(pos * CHUNK, CHUNK), CHUNK)
    land_v[mine_rows] = send_v[mine_rows]
    pl.semaphore_wait(barrier, 2 * POS - 1 + 6)

    def copy(src, dst, i, p, l, h):
        return pltpu.make_async_remote_copy(
            src_ref=src, dst_ref=dst, send_sem=ssem.at[i], recv_sem=rsem.at[i],
            device_id=(p * LANES + l, h), device_id_type=MESH,
        )

    def done(ref, sem):
        pltpu.make_async_copy(ref, ref, sem).wait()

    sel = lax.rem(pos + core, 2)
    giver = sel == half
    loads[3].wait()
    copy(texts, land_r.at[half], 8, pos, cross, sel).start()
    drains.append(lambda: done(texts, ssem.at[8]))
    for dy, dx in STEPS:
        p = at(dy, dx)
        copy(send_s.at[p], land_s.at[pos], 1, p, lane, other).start()
    for dy, dx in STEPS[:-1]:
        p = at(dy, dx)
        copy(
            send_v.at[pl.ds(pl.multiple_of(p * CHUNK, CHUNK), CHUNK)],
            land_v.at[mine_rows], 0, p, lane, half,
        ).start()
    drains.append(lambda: done(send_v.at[pl.ds(0, (POS - 1) * CHUNK)], ssem.at[0]))
    drains.append(lambda: done(send_s, ssem.at[1]))

    @pl.when(giver)
    def _():
        done(land_r, rsem.at[8])
        for dy, dx in STEPS[:8]:
            copy(land_r, land_x.at[pos // 2], 2, at(dy, dx), lane, half).start()
        land_x[pos // 2] = land_r[...]

    def handed():
        @pl.when(giver)
        def _():
            done(land_x, ssem.at[2])
            done(land_x.at[pl.ds(0, BLK - 1)], ssem.at[2])

    drains.append(handed)

    done(land_v.at[pl.ds(0, (POS - 1) * CHUNK)], rsem.at[0])
    held = land_v[...]
    second = (lax.broadcasted_iota(jnp.int32, (1, POS * CHUNK), 1) & SLOTS) != 0
    piece = nt(ask, held)
    piece = jnp.where(second, piece[SLOTS : SLOTS + 1], piece[:1])
    rest = jnp.where(second, pltpu.roll(piece, SLOTS, 1), pltpu.roll(piece, POS * CHUNK - SLOTS, 1))

    @pl.when(giver)
    def _():
        for dy, dx in STEPS[8:-1]:
            copy(land_r, land_x.at[pos // 2], 2, at(dy, dx), lane, half).start()

    done(land_s, rsem.at[1])
    more = jnp.sum(land_s[...].reshape(2, 8, 2, 128), axis=1)
    more = jnp.concatenate([more[0], more[1]], axis=1)
    weight = jax.nn.sigmoid(piece + rest + more[:1]).astype(BF).astype(F32)
    study_row = (wide_row & (COL - 1)) + 1
    fits = (more[1:] == study_row.astype(F32)) & (((wide_row & COL) != 0) == ((wide_col & SLOTS) != 0))
    table = jnp.where(fits, weight, 0.0).astype(BF)
    sums = jnp.dot(table, held, preferred_element_type=F32)
    total = jnp.dot(table[:COL], jnp.ones((POS * CHUNK, 128), BF), preferred_element_type=F32)
    sums = jnp.concatenate([sums[:COL], sums[COL:], total], axis=1)
    part[...] = sums.astype(BF)
    sib = copy(part, land_sib, 3, pos, lane + 1 - 2 * core, half)
    sib.start()
    sib.wait_recv()
    drains.append(sib.wait_send)
    col_sum[...] = (sums + land_sib[...].astype(F32)).astype(BF)
    z = half * 2 + zlo
    for k in (2, 1, 3):
        there = lax.rem(z + k, 4)
        copy(
            col_sum.at[:, pl.ds(0, WIDTH)], land_sum.at[z], 4, pos, lax.rem(there, 2) * 2 + core, there // 2
        ).start()
    copy(col_sum.at[:, pl.ds(WIDTH, 128)], land_den, 7, pos, cross, half).start()
    land_sum[z] = col_sum[:, :WIDTH]
    drains.append(lambda: done(land_sum.at[pl.ds(0, 3)], ssem.at[4]))
    drains.append(lambda: done(land_den, ssem.at[7]))

    @pl.when(giver)
    def _():
        done(land_x.at[pl.ds(0, BLK - 1)], rsem.at[2])

    @pl.when(jnp.logical_not(giver))
    def _():
        done(land_x, rsem.at[2])

    raw = [land_x[:, h].reshape(REP, WIDTH).astype(F32) for h in range(HALVES)]
    norm = jnp.sum(raw[0] * raw[0] + raw[1] * raw[1], axis=1, keepdims=True)
    inv = lax.rsqrt(norm + 1e-06)
    report = jnp.concatenate([(x * inv).astype(BF) for x in raw], axis=1)

    done(land_den, rsem.at[7])
    done(land_sum.at[pl.ds(0, 3)], rsem.at[4])
    both = [
        land_sum[2 * h].astype(F32) + land_sum[2 * h + 1].astype(F32) for h in range(HALVES)
    ]
    weights = col_sum[:, WIDTH:].astype(F32) + land_den[...].astype(F32)
    share = 1.0 / weights[:, :1]
    mean = [x * share for x in both]
    norm = jnp.sum(mean[0] * mean[0] + mean[1] * mean[1], axis=1, keepdims=True)
    inv = lax.rsqrt(norm + 1e-06)
    unit = jnp.concatenate([(x * inv).astype(BF) for x in mean], axis=1)

    logits = scale[0] * nt(report, unit) + bias[0]
    i = lax.broadcasted_iota(jnp.int32, (REP, COL), 1)
    j = lax.broadcasted_iota(jnp.int32, (REP, COL), 0)
    study_id = pos * COL + i
    report_id = ((2 * (j // OWN) + lax.rem(half + core, 2)) * LANES + cross) * OWN + lax.rem(j, OWN)
    own = (study_id == report_id).astype(F32)
    slope = (jax.nn.sigmoid(logits) - own).astype(BF)

    odd = lax.rem(px + half + core, 2)
    odd_column = lax.rem(half + core, 2)
    given = [(y, lax.rem(px + dx + odd, SIDE)) for y in (rows_of[2], rows_of[1], rows_of[3], rows_of[0]) for dx in (2, 0)]
    for h in (0,):
        text_part[h] = jnp.dot(slope, unit[:, h * WIDTH : (h + 1) * WIDTH], preferred_element_type=F32).astype(BF)
        for y, x in given:
            rows = pl.ds(pl.multiple_of((y + x - odd_column) * BLK, OWN), OWN)
            copy(text_part.at[h, rows], land_t.at[pos], 5, y + x, cross, h).start()
    drains.append(lambda: done(land_t, ssem.at[5]))

    gp = tn(slope, report).astype(BF)
    for h in range(HALVES):
        pooled_part[h] = gp[:, h * WIDTH : (h + 1) * WIDTH].reshape(2, CORES, OWN, WIDTH)
    pair = copy(pooled_part.at[:, :, 1 - core], land_q, 9, pos, lane + 1 - 2 * core, half)
    pair.start()
    for h in (1,):
        text_part[h] = jnp.dot(slope, unit[:, h * WIDTH : (h + 1) * WIDTH], preferred_element_type=F32).astype(BF)
        for y, x in given:
            rows = pl.ds(pl.multiple_of((y + x - odd_column) * BLK, OWN), OWN)
            copy(text_part.at[h, rows], land_t.at[pos], 5, y + x, cross, h).start()
    drains.append(pair.wait_send)
    pair.wait_recv()
    pooled_sum[...] = (pooled_part[:, :, core].astype(F32) + land_q[...].astype(F32)).astype(BF)
    for k in (2, 1, 3):
        there = lax.rem(z + k, 4)
        h, l = lax.div(there, 2), lax.rem(there, 2)
        copy(pooled_sum.at[h, l], land_p.at[z], 6, pos, l * 2 + core, h).start()
    land_p[z] = pooled_sum[half, zlo]
    drains.append(lambda: done(land_p.at[pl.ds(0, 3)], ssem.at[6]))

    done(land_p.at[pl.ds(0, 3)], rsem.at[6])
    out_pooled[1] = jnp.zeros((OWN, WIDTH), BF)
    out_text[1] = jnp.zeros((OWN, WIDTH), BF)
    out_pooled[0] = jnp.sum(land_p[...].astype(F32), axis=0).astype(BF)
    for drain in drains:
        drain()
    done(land_t, rsem.at[5])
    out_text[0] = jnp.sum(land_t[...].astype(F32), axis=0).astype(BF)


def on_device(views, view_study, pool_query, texts, logit_scale, logit_bias):
    slots = views.shape[0]
    vmem = pl.BlockSpec(memory_space=pltpu.VMEM)
    hbm = pl.BlockSpec(memory_space=pltpu.HBM)
    smem = pl.BlockSpec(memory_space=pltpu.SMEM)
    out = jax.ShapeDtypeStruct((2, OWN, WIDTH), BF)
    res = pl.pallas_call(
        kernel,
        out_shape=(out, out),
        in_specs=[hbm, hbm, hbm, hbm, smem, smem],
        out_specs=(vmem, vmem),
        scratch_shapes=[
            pltpu.VMEM((slots, WIDTH), BF),
            pltpu.VMEM((1, slots), jnp.int32),
            pltpu.VMEM((WIDTH,), BF),
            pltpu.VMEM((OWN, WIDTH), BF),
            pltpu.VMEM((POS * CHUNK, PIECE), BF),
            pltpu.VMEM((POS * CHUNK, PIECE), BF),
            pltpu.VMEM((POS, 2, 128), F32),
            pltpu.VMEM((POS, 2, 128), F32),
            pltpu.VMEM((HALVES, OWN, WIDTH), BF),
            pltpu.VMEM((BLK, HALVES, OWN, WIDTH), BF),
            pltpu.VMEM((COL, WIDE), BF),
            pltpu.VMEM((COL, WIDE), BF),
            pltpu.VMEM((COL, WIDE), BF),
            pltpu.VMEM((4, COL, WIDTH), BF),
            pltpu.VMEM((COL, 128), BF),
            pltpu.VMEM((HALVES, REP, WIDTH), BF),
            pltpu.VMEM((HALVES, 2, CORES, OWN, WIDTH), BF),
            pltpu.VMEM((HALVES, 2, OWN, WIDTH), BF),
            pltpu.VMEM((HALVES, 2, OWN, WIDTH), BF),
            pltpu.VMEM((POS, OWN, WIDTH), BF),
            pltpu.VMEM((4, OWN, WIDTH), BF),
            pltpu.SemaphoreType.DMA((10,)),
            pltpu.SemaphoreType.DMA((10,)),
            pltpu.SemaphoreType.DMA((4,)),
        ],
        compiler_params=pltpu.CompilerParams(
            collective_id=0, has_side_effects=True, vmem_limit_bytes=32 << 20
        ),
    )(
        *(pltpu.with_memory_space_constraint(x, pltpu.HBM) for x in (views, view_study.reshape(1, slots), pool_query, texts)),
        logit_scale, logit_bias,
    )
    zero = jnp.zeros((), BF)
    return tuple(
        lax.reduce(tuple(res), (zero, zero), lambda a, b: (a[0] + b[0], a[1] + b[1]), (0,))
    )


def solution(mesh):
    in_specs = (P("dp", "mp"), P("dp"), P("mp"), P("dp", "mp"), P(), P())
    out_specs = (P("dp", "mp"), P("dp", "mp"))
    return jax.shard_map(
        on_device, mesh=mesh, in_specs=in_specs, out_specs=out_specs, check_vma=False
    )
```
